256 devices in a mesh: section: 8 (over z_hi, x), expert: 32 (over z_lo, y, core).
Axes of the slice: x: 4, y: 4, z: 8 (z_hi: 2, z_lo: 4; z = z_hi * 4 + z_lo), core: 2. Of those that a mesh axis runs over, the one named last changes fastest.
Arguments:
- x_a: bfloat16 [32768, 7168], P(('section', 'expert')), may hold values from -6 to 6
- routes_a: int32 [32768], P(('section', 'expert')), may hold values from 0 to 4, as said below
- scale_a: float32 [32768], P(('section', 'expert')), may hold values from 0.1 to 1
- cotangent_b: bfloat16 [32768, 7168], P(('section', 'expert')), may hold values from -6 to 6
- routes_b: int32 [32768], P(('section', 'expert')), may hold values from 0 to 4, as said below
- scale_b: float32 [32768], P(('section', 'expert')), may hold values from 0.1 to 1
- saved_b: bfloat16 [32768, 2048], P(('section', 'expert')), may hold values from -6 to 6
- w_gate_up: bfloat16 [229376, 2048], P(('section', 'expert')), may hold values from -0.0625 to 0.0625
- w_down_t: bfloat16 [229376, 1024], P(('section', 'expert')), may hold values from -0.1875 to 0.1875
Outputs:
- handoff: bfloat16 [32768, 7168], P(('section', 'expert'))
- grad_handoff: bfloat16 [32768, 7168], P(('section', 'expert'))
The draws below stay inside these ranges and needn't reach their ends.
Inputs may be any that keep to these rules, and one draw needn't show every extreme that they name: `routes_a`: 4 means that the token's route leads to an expert outside this window. Among the 128 tokens of one device no value below 4 occurs more than 12 times, and in every draw some value occurs exactly 12 times on every device. `routes_b`: as routes_a.
All inputs are finite; a program needn't handle non-finite values.
Results may differ from the reference program's by a relative error of at most 0.002.
Values may be sent and summed in bfloat16 or wider, within the bound.
A program may use at most 128 MiB of HBM per device.

```python
import math
import jax
import jax.numpy as jnp

D = 7168
FF = 1024
CAP = 12
TOK_DEV = 128
EXPERTS = 4
TOKENS = 4096
N_SECTION = 8
N_EXPERT = 32


def route_table(key):
    blocks = N_SECTION * TOKENS // TOK_DEV
    key_full, key_count, key_order = jax.random.split(key, 3)
    full_expert = jax.random.randint(key_full, (), 0, EXPERTS)
    counts = jax.random.randint(key_count, (blocks, EXPERTS), 1, CAP + 1)
    counts = jnp.where(jnp.arange(EXPERTS)[None, :] == full_expert, CAP, counts)
    bounds = jnp.cumsum(counts, axis=1)
    position = jnp.arange(TOK_DEV)
    owner = jnp.sum((position[None, :, None] >= bounds[:, None, :]).astype(jnp.int32), axis=2)
    order_keys = jax.random.split(key_order, blocks)
    orders = jax.vmap(lambda single: jax.random.permutation(single, TOK_DEV))(order_keys)
    routes = jnp.take_along_axis(owner, orders, axis=1)
    return routes.reshape(-1).astype(jnp.int32)


def draw_routes_a(key, part):
    key = jax.random.fold_in(key, 11)
    return route_table(key)


def draw_routes_b(key, part):
    key = jax.random.fold_in(key, 23)
    return route_table(key)


def levels(own_key, extent, shards, low, high):
    level, own = 1.0, jax.random.fold_in(own_key, 6)
    for dim, blocks in shards:
        draws = jnp.exp(jax.random.uniform(jax.random.fold_in(own, dim), (blocks,), jnp.float32, low / len(shards), high / len(shards)))
        level = level * jnp.repeat(draws, extent[dim] // blocks).reshape([-1 if axis == dim else 1 for axis in range(len(extent))])
    return level


def noise(key, extent, spread, most, cuts=(), held_as=jnp.bfloat16):
    level = levels(key, extent, cuts, -0.22, 0.18) if cuts else 1.0
    values = jax.random.normal(key, extent, jnp.float32) * spread * level
    return jnp.minimum(jnp.maximum(values, -most), most).astype(held_as)


def setup_inputs(seed: int = 0) -> dict:
    arg_keys = jax.random.split(jax.random.key(seed), 10)
    return {
        "x_a": noise(arg_keys[0], (N_SECTION * TOKENS, D), 1.0, 6.0, ((0, 256),)),
        "routes_a": draw_routes_a(jax.random.fold_in(arg_keys[9], 71), 0),
        "scale_a": jnp.clip(jnp.exp(math.log(1.0) - 2.3025851 * jax.random.uniform(arg_keys[2], (N_SECTION * TOKENS,), jnp.float32) ** levels(arg_keys[2], (N_SECTION * TOKENS,), ((0, 256),), -0.2, 0.2)), 0.1, 1.0),
        "cotangent_b": noise(arg_keys[3], (N_SECTION * TOKENS, D), 1.0, 6.0, ((0, 256),)),
        "routes_b": draw_routes_b(jax.random.fold_in(arg_keys[9], 71), 0),
        "scale_b": jnp.clip(jnp.exp(math.log(1.0) - 2.3025851 * jax.random.uniform(arg_keys[5], (N_SECTION * TOKENS,), jnp.float32) ** levels(arg_keys[5], (N_SECTION * TOKENS,), ((0, 256),), -0.2, 0.2)), 0.1, 1.0),
        "saved_b": noise(arg_keys[6], (N_SECTION * TOKENS, 2 * FF), 1.0, 6.0, ((0, 256),)),
        "w_gate_up": noise(arg_keys[7], (N_SECTION * EXPERTS * D, 2 * FF), D ** -0.5, 0.0625, ((0, 256),)),
        "w_down_t": noise(arg_keys[8], (N_SECTION * EXPERTS * D, FF), FF ** -0.5, 0.1875, ((0, 256),)),
    }


def expert_rows(routes, expert):
    chosen = routes == expert
    limit = CAP * N_EXPERT
    index = jnp.nonzero(chosen, size=limit, fill_value=0)[0].astype(jnp.int32)
    valid = jnp.arange(limit, dtype=jnp.int32) < jnp.sum(chosen.astype(jnp.int32))
    return index, valid


def silu_grads(dhidden, saved_rows):
    pre_gate = saved_rows[:, :FF].astype(jnp.float32)
    pre_up = saved_rows[:, FF:].astype(jnp.float32)
    sigmoid_gate = jax.nn.sigmoid(pre_gate)
    grad_gate = dhidden * pre_up * sigmoid_gate * (1.0 + pre_gate * (1.0 - sigmoid_gate))
    grad_up = dhidden * pre_gate * sigmoid_gate
    return jnp.concatenate([grad_gate, grad_up], axis=1).astype(jnp.bfloat16)


def reference(x_a, routes_a, scale_a, cotangent_b, routes_b, scale_b, saved_b, w_gate_up, w_down_t):
    forward_list = []
    backward_list = []
    for section in range(N_SECTION):
        first = section * EXPERTS * D
        gate_up = w_gate_up[first:first + EXPERTS * D].reshape(EXPERTS, D, 2 * FF)
        down_t = w_down_t[first:first + EXPERTS * D].reshape(EXPERTS, D, FF)
        begin = section * TOKENS
        tokens = x_a[begin:begin + TOKENS]
        route_fwd = routes_a[begin:begin + TOKENS]
        route_bwd = routes_b[begin:begin + TOKENS]
        cotangent = cotangent_b[begin:begin + TOKENS]
        saved_rows = saved_b[begin:begin + TOKENS]
        scaled = (scale_b[begin:begin + TOKENS][:, None] * cotangent.astype(jnp.float32)).astype(jnp.bfloat16)
        combined = jnp.zeros((TOKENS, D), jnp.float32)
        grad_sum = jnp.zeros((TOKENS, D), jnp.float32)
        for expert in range(EXPERTS):
            index, valid = expert_rows(route_fwd, expert)
            projected = jnp.dot(tokens[index], gate_up[expert], preferred_element_type=jnp.float32)
            hidden = (jax.nn.silu(projected[:, :FF]) * projected[:, FF:]).astype(jnp.bfloat16)
            expert_out = jnp.dot(hidden, down_t[expert].T, preferred_element_type=jnp.float32)
            expert_out = expert_out.astype(jnp.bfloat16).astype(jnp.float32)
            combined = combined.at[index].add(jnp.where(valid[:, None], expert_out, 0.0))
            index_b, valid_b = expert_rows(route_bwd, expert)
            dhidden = jnp.dot(scaled[index_b], down_t[expert], preferred_element_type=jnp.float32)
            gate_grads = silu_grads(dhidden, saved_rows[index_b])
            expert_grad = jnp.dot(gate_grads, gate_up[expert].T, preferred_element_type=jnp.float32)
            expert_grad = expert_grad.astype(jnp.bfloat16).astype(jnp.float32)
            grad_sum = grad_sum.at[index_b].add(jnp.where(valid_b[:, None], expert_grad, 0.0))
        forward_out = (tokens.astype(jnp.float32) + scale_a[begin:begin + TOKENS][:, None] * combined).astype(jnp.bfloat16)
        input_grad = (cotangent.astype(jnp.float32) + grad_sum).astype(jnp.bfloat16)
        forward_list.append(forward_out)
        backward_list.append(input_grad)
    handoff = jnp.roll(jnp.stack(forward_list), 1, axis=0).reshape(N_SECTION * TOKENS, D)
    grad_handoff = jnp.roll(jnp.stack(backward_list), -1, axis=0).reshape(N_SECTION * TOKENS, D)
    return (handoff, grad_handoff)
```

```python
import functools

import jax
import jax.numpy as jnp
import numpy as np
from jax import lax
from jax.experimental import pallas as pl
from jax.experimental.pallas import tpu as pltpu
from jax.sharding import PartitionSpec as P

FF = 1024
GROUP = 8
CAP = 12
EXPERTS = 4
SLOTS = EXPERTS * CAP
TOK = 128
EARLY = TOK - SLOTS
D = 7168
SL = D // GROUP
HC = FF // GROUP
ROWS = GROUP * SLOTS
ZROWS = GROUP * CAP
BF = jnp.bfloat16
F32 = jnp.float32
SUM_T = jnp.bfloat16
PAIRS = [(2, 0), (2, 1), (1, 0), (1, 1), (3, 0), (3, 1), (0, 1)]


def regroup_matrix():
    row = np.arange(ROWS)
    expert, peer, slot = row // ZROWS, (row % ZROWS) // CAP, row % CAP
    column = peer * SLOTS + expert * CAP + slot
    table = np.zeros((ROWS, ROWS), np.float32)
    table[row, column] = 1.0
    return table


def nt_dot(left, right):
    return lax.dot_general(left, right, (((1,), (1,)), ((), ())), preferred_element_type=F32)


def nn_dot(left, right):
    return jnp.dot(left, right, preferred_element_type=F32)


def iota(shape, dim):
    return lax.broadcasted_iota(jnp.int32, shape, dim)


def slot_positions(routes):
    match = (routes == iota((8, TOK), 0)).astype(F32)
    upper = (iota((TOK, TOK), 0) <= iota((TOK, TOK), 1)).astype(BF)
    rank = nn_dot(match.astype(BF), upper) - 1.0
    counts = jnp.sum(match, axis=1, keepdims=True)
    spare = rank[EXPERTS : EXPERTS + 1] - EARLY
    placed = jnp.zeros((1, TOK), F32)
    leftover = jnp.zeros((1, TOK), F32)
    before = jnp.zeros((1, 1), F32)
    for expert in range(EXPERTS):
        own = match[expert : expert + 1]
        count = counts[expert : expert + 1]
        placed = placed + own * (CAP * expert + rank[expert : expert + 1])
        after = before + (CAP - count)
        inside = (spare >= before) & (spare < after)
        leftover = leftover + jnp.where(inside, CAP * expert + count + (spare - before), 0.0)
        before = after
    outside = jnp.where(spare < 0.0, spare + TOK, leftover)
    return placed + match[EXPERTS : EXPERTS + 1] * outside


def slot_matrix(routes, scale):
    pos = slot_positions(routes)
    hit = iota((TOK, TOK), 0).astype(F32) == pos
    kept = jnp.where(routes < EXPERTS, scale, 0.0)
    column = jnp.sum(jnp.where(hit, kept, 0.0), axis=1, keepdims=True)
    eye = iota((TOK, TOK), 0) == iota((TOK, TOK), 1)
    row = jnp.sum(jnp.where(eye, column, 0.0), axis=0, keepdims=True)
    return hit.astype(BF), row


def kernel(
    routes_a, scale_a, routes_b, scale_b, x_hbm, cot_hbm, saved_hbm, wgu_hbm, wd_hbm, regroup_hbm,
    rows_a, rows_b, perm_a, perm_b,
    x_v, cot_v, saved_v, wgu, wd, regroup,
    pm_a, pm_b, sc_out, sc_in,
    pk_a, pk_b, early_a, early_b,
    r1_a, r1_b, s2_a, s2_b, r2_a, r2_b,
    ps_a, ps_b, own_a, own_b, rs_a, rs_b,
    h_a, g_b, eo_a, eo_b, r3_a, r3_b, s4_a, s4_b,
    load_sem,
    sc_ss, sc_rs, d1a_ss, d1a_rs, d1b_ss, d1b_rs, d2a_ss, d2a_rs, d2b_ss, d2b_rs,
    rsa_ss, rsa_rs, rsb_ss, rsb_rs, aga_ss, aga_rs, agb_ss, agb_rs,
    rta_ss, rta_rs, rtb_ss, rtb_rs, fa_ss, fa_rs, fb_ss, fb_rs, e_ss, e_rs,
):
    section = lax.axis_index("section")
    place = lax.axis_index("expert")
    layer = place // GROUP
    me = place % GROUP
    y = me // 2
    core = me % 2
    n_sec = lax.axis_size("section")
    ahead = (section + 1) % n_sec
    behind = (section + n_sec - 1) % n_sec

    def peer(pair):
        return ((y + pair[0]) % 4) * 2 + (core + pair[1]) % 2

    def plane_dev(pair):
        return (section, layer * GROUP + peer(pair))

    def depth(step):
        return (layer + step) % EXPERTS

    def depth_dev(step):
        return (section, depth(step) * GROUP + me)

    def remote(src, dst, ss, rs, dev):
        return pltpu.make_async_remote_copy(
            src_ref=src, dst_ref=dst, send_sem=ss, recv_sem=rs,
            device_id=dev, device_id_type=pl.DeviceIdType.MESH,
        )

    barrier = pltpu.get_barrier_semaphore()
    greeted = [plane_dev(pair) for pair in PAIRS] + [depth_dev(step) for step in (1, 2, 3)]
    for other in range(GROUP):
        greeted.append((ahead, layer * GROUP + other))
        greeted.append((behind, layer * GROUP + other))
    for dev in greeted:
        pl.semaphore_signal(barrier, 1, device_id=dev, device_id_type=pl.DeviceIdType.MESH)

    loads = []
    for i, (src, dst) in enumerate(
        [(x_hbm, x_v), (cot_hbm, cot_v), (saved_hbm, saved_v), (regroup_hbm, regroup),
         (wgu_hbm, wgu), (wd_hbm, wd)]
    ):
        copy = pltpu.make_async_copy(src, dst, load_sem.at[i])
        copy.start()
        loads.append(copy)

    mat_a, row_a = slot_matrix(routes_a[...], scale_a[...])
    mat_b, row_b = slot_matrix(routes_b[...], scale_b[...])
    pm_a[...] = mat_a
    pm_b[...] = mat_b
    line = iota((8, TOK), 0)
    sc_out[...] = jnp.where(line == 0, row_a, jnp.where(line == 1, row_b, 0.0))
    sc_in[me] = sc_out[...]

    pending = []

    loads[0].wait()
    for part in range(GROUP):
        cols = slice(part * SL, (part + 1) * SL)
        packed = nn_dot(pm_a[...], x_v[:, cols]).astype(BF)
        pk_a[part] = packed[:SLOTS]
        early_a[:, cols] = packed[SLOTS:]
    pl.semaphore_wait(barrier, len(greeted))

    def plane_sends(items):
        out = []
        for i, pair in enumerate(PAIRS):
            for src, dst, ss, rs in items(pair):
                copy = remote(src, dst, ss.at[i], rs.at[i], plane_dev(pair))
                copy.start()
                out.append(copy)
                pending.append(copy)
        return out

    in_1a = plane_sends(lambda pair: [
        (pk_a.at[peer(pair)], r1_a.at[me], d1a_ss, d1a_rs),
        (sc_out, sc_in.at[me], sc_ss, sc_rs),
    ])
    r1_a[me] = pk_a[me]

    loads[1].wait()
    loads[2].wait()
    for part in range(GROUP):
        cols = slice(part * SL, (part + 1) * SL)
        packed = nn_dot(pm_b[...], cot_v[:, cols]).astype(BF)
        pk_b[part, :, :SL] = packed[:SLOTS]
        early_b[:, cols] = packed[SLOTS:]
        for half in range(2):
            first = half * FF + part * HC
            picked = nn_dot(pm_b[:SLOTS, :], saved_v[:, first : first + HC]).astype(BF)
            pk_b[part, :, SL + half * HC : SL + (half + 1) * HC] = picked
    in_1b = plane_sends(lambda pair: [(pk_b.at[peer(pair)], r1_b.at[me], d1b_ss, d1b_rs)])
    r1_b[me] = pk_b[me]

    def scale_column(which):
        mask = iota((SLOTS, TOK), 0) == iota((SLOTS, TOK), 1)
        return [
            jnp.sum(jnp.where(mask, sc_in[p, which : which + 1, :], 0.0), axis=1, keepdims=True)
            for p in range(GROUP)
        ]

    def depth_sends(src, dst, ss, rs):
        out = []
        for i, step in enumerate((2, 1, 3)):
            copy = remote(src.at[depth(step)], dst.at[layer], ss.at[i], rs.at[i], depth_dev(step))
            copy.start()
            out.append(copy)
            pending.append(copy)
        return out

    for copy in in_1a:
        copy.wait_recv()
    loads[3].wait()
    moved = nn_dot(regroup[...], r1_a[...].reshape(ROWS, SL)).astype(BF)
    s2_a[...] = moved.reshape(EXPERTS, ZROWS, SL)
    in_2a = depth_sends(s2_a, r2_a, d2a_ss, d2a_rs)
    r2_a[layer] = s2_a[layer]

    for copy in in_1b:
        copy.wait_recv()
    columns = scale_column(1)
    scaled = jnp.concatenate(
        [(columns[p] * r1_b[p, :, :SL].astype(F32)).astype(BF) for p in range(GROUP)], axis=0
    )
    s2_b[:, :, :SL] = nn_dot(regroup[...], scaled).astype(BF).reshape(EXPERTS, ZROWS, SL)
    carried = r1_b[:, :, SL:].reshape(ROWS, 2 * HC)
    s2_b[:, :, SL:] = nn_dot(regroup[...], carried).astype(BF).reshape(EXPERTS, ZROWS, 2 * HC)
    in_2b = depth_sends(s2_b, r2_b, d2b_ss, d2b_rs)
    r2_b[layer] = s2_b[layer]

    finals = []
    for i, (src, dst, sec) in enumerate([
        (early_a, rows_a.at[pl.ds(SLOTS, EARLY), :], ahead),
        (early_b, rows_b.at[pl.ds(SLOTS, EARLY), :], behind),
        (pm_a, perm_a, ahead),
        (pm_b, perm_b, behind),
    ]):
        copy = remote(src, dst, e_ss.at[i], e_rs.at[i], (sec, place))
        copy.start()
        finals.append(copy)
        pending.append(copy)

    for copy in in_2a:
        copy.wait_recv()
    loads[4].wait()
    loads[5].wait()
    in_rsa = []
    for i, d in enumerate((2, 1, 3, 0)):
        chip = (y + d) % 4
        acts = r2_a[...].reshape(ROWS, SL)
        first = pl.multiple_of(chip * (2 * HC), 2 * HC)
        gate = nn_dot(acts, wgu[:, pl.ds(first, 2 * HC)])
        second = pl.multiple_of(FF + chip * (2 * HC), 2 * HC)
        up = nn_dot(acts, wgu[:, pl.ds(second, 2 * HC)])
        for c in range(2):
            cols = slice(c * HC, (c + 1) * HC)
            ps_a[d, c, :, :HC] = gate[:, cols].astype(SUM_T)
            ps_a[d, c, :, HC:] = up[:, cols].astype(SUM_T)
            if d == 0:
                own_a[c, :, :HC] = gate[:, cols]
                own_a[c, :, HC:] = up[:, cols]
        for cc in range(2):
            if (d, cc) != (0, 0):
                k = PAIRS.index((d, cc))
                copy = remote(ps_a.at[d, (core + cc) % 2], rs_a.at[k], rsa_ss.at[k], rsa_rs.at[k], plane_dev((d, cc)))
                copy.start()
                in_rsa.append(copy)
                pending.append(copy)

    for copy in in_2b:
        copy.wait_recv()
    in_rsb = []
    for i, d in enumerate((2, 1, 3, 0)):
        chip = (y + d) % 4
        acts = r2_b[:, :, :SL].reshape(ROWS, SL)
        first = pl.multiple_of(chip * (2 * HC), 2 * HC)
        part = nn_dot(acts, wd[:, pl.ds(first, 2 * HC)])
        for c in range(2):
            cols = slice(c * HC, (c + 1) * HC)
            ps_b[d, c] = part[:, cols].astype(SUM_T)
            if d == 0:
                own_b[c] = part[:, cols]
        for cc in range(2):
            if (d, cc) != (0, 0):
                k = PAIRS.index((d, cc))
                copy = remote(ps_b.at[d, (core + cc) % 2], rs_b.at[k], rsb_ss.at[k], rsb_rs.at[k], plane_dev((d, cc)))
                copy.start()
                in_rsb.append(copy)
                pending.append(copy)

    for copy in in_rsa:
        copy.wait_recv()
    total = own_a[core]
    for k in range(len(PAIRS)):
        total = total + rs_a[k].astype(F32)
    gate, up = total[:, :HC], total[:, HC:]
    h_a[me] = (gate * jax.nn.sigmoid(gate) * up).astype(BF)
    in_aga = plane_sends(lambda pair: [(h_a.at[me], h_a.at[me], aga_ss, aga_rs)])

    for copy in in_rsb:
        copy.wait_recv()
    dhid = own_b[core]
    for k in range(len(PAIRS)):
        dhid = dhid + rs_b[k].astype(F32)
    held = r2_b[:, :, SL:].reshape(ROWS, 2 * HC).astype(F32)
    gate, up = held[:, :HC], held[:, HC:]
    sig = jax.nn.sigmoid(gate)
    g_b[me, :, :HC] = (dhid * up * sig * (1.0 + gate * (1.0 - sig))).astype(BF)
    g_b[me, :, HC:] = (dhid * gate * sig).astype(BF)
    in_agb = plane_sends(lambda pair: [(g_b.at[me], g_b.at[me], agb_ss, agb_rs)])

    for copy in in_aga:
        copy.wait_recv()
    hidden = jnp.concatenate([h_a[p] for p in range(GROUP)], axis=1)
    for q in range(0, SL, 128):
        out = nt_dot(hidden, wd[q : q + 128, :]).astype(BF)
        eo_a[:, :, q : q + 128] = out.reshape(EXPERTS, ZROWS, 128)
    in_3a = depth_sends(eo_a, r3_a, rta_ss, rta_rs)
    r3_a[layer] = eo_a[layer]

    for copy in in_agb:
        copy.wait_recv()
    left = jnp.concatenate([g_b[p, :, :HC] for p in range(GROUP)], axis=1)
    right = jnp.concatenate([g_b[p, :, HC:] for p in range(GROUP)], axis=1)
    for q in range(0, SL, 128):
        out = nt_dot(left, wgu[q : q + 128, :FF]) + nt_dot(right, wgu[q : q + 128, FF:])
        eo_b[:, :, q : q + 128] = out.astype(BF).reshape(EXPERTS, ZROWS, 128)
    in_3b = depth_sends(eo_b, r3_b, rtb_ss, rtb_rs)
    r3_b[layer] = eo_b[layer]

    def last_sends(src, dst, ss, rs, sec):
        lane = pl.multiple_of(me * SL, SL)
        for p in range(GROUP):
            other = (me + p) % GROUP
            copy = remote(
                src.at[other], dst.at[pl.ds(0, SLOTS), pl.ds(lane, SL)],
                ss.at[p], rs.at[p], (sec, layer * GROUP + other),
            )
            copy.start()
            finals.append(copy)
            pending.append(copy)

    def back(ref):
        return lax.dot_general(
            regroup[...], ref[...].reshape(ROWS, SL), (((0,), (0,)), ((), ())),
            preferred_element_type=F32,
        ).reshape(GROUP, SLOTS, SL)

    for copy in in_3a:
        copy.wait_recv()
    columns = scale_column(0)
    came = back(r3_a)
    for p in range(GROUP):
        s4_a[p] = (r1_a[p].astype(F32) + columns[p] * came[p]).astype(BF)
    last_sends(s4_a, rows_a, fa_ss, fa_rs, ahead)

    for copy in in_3b:
        copy.wait_recv()
    came = back(r3_b)
    for p in range(GROUP):
        s4_b[p] = (r1_b[p, :, :SL].astype(F32) + came[p]).astype(BF)
    last_sends(s4_b, rows_b, fb_ss, fb_rs, behind)

    for copy in finals:
        copy.wait_recv()
    for copy in pending:
        copy.wait_send()


def relay_layer(routes_a, scale_a, routes_b, scale_b, x, cot, saved, wgu, wd):
    vmem, hbm = pl.BlockSpec(memory_space=pltpu.VMEM), pl.BlockSpec(memory_space=pl.ANY)
    dma = pltpu.SemaphoreType.DMA
    v = pltpu.VMEM
    n = len(PAIRS)
    wide = SL + 2 * HC
    scratch = [
        v((TOK, D), BF), v((TOK, D), BF), v((TOK, 2 * FF), BF), v((SL, 2 * FF), BF), v((SL, FF), BF), v((ROWS, ROWS), BF),
        v((TOK, TOK), BF), v((TOK, TOK), BF), v((8, TOK), F32), v((GROUP, 8, TOK), F32),
        v((GROUP, SLOTS, SL), BF), v((GROUP, SLOTS, wide), BF), v((EARLY, D), BF), v((EARLY, D), BF),
        v((GROUP, SLOTS, SL), BF), v((GROUP, SLOTS, wide), BF),
        v((EXPERTS, ZROWS, SL), BF), v((EXPERTS, ZROWS, wide), BF),
        v((EXPERTS, ZROWS, SL), BF), v((EXPERTS, ZROWS, wide), BF),
        v((4, 2, ROWS, 2 * HC), SUM_T), v((4, 2, ROWS, HC), SUM_T), v((2, ROWS, 2 * HC), F32), v((2, ROWS, HC), F32),
        v((n, ROWS, 2 * HC), SUM_T), v((n, ROWS, HC), SUM_T),
        v((GROUP, ROWS, HC), BF), v((GROUP, ROWS, 2 * HC), BF),
        v((EXPERTS, ZROWS, SL), BF), v((EXPERTS, ZROWS, SL), BF),
        v((EXPERTS, ZROWS, SL), BF), v((EXPERTS, ZROWS, SL), BF),
        v((GROUP, SLOTS, SL), BF), v((GROUP, SLOTS, SL), BF),
        dma((6,)),
    ]
    for size in (n, n, n, 3, 3, n, n, n, n, 3, 3, GROUP, GROUP, 4):
        scratch += [dma((size,)), dma((size,))]
    return pl.pallas_call(
        kernel,
        out_shape=[
            jax.ShapeDtypeStruct((TOK, D), BF), jax.ShapeDtypeStruct((TOK, D), BF),
            jax.ShapeDtypeStruct((TOK, TOK), BF), jax.ShapeDtypeStruct((TOK, TOK), BF),
        ],
        in_specs=[vmem] * 4 + [hbm] * 6,
        out_specs=[hbm] * 4,
        scratch_shapes=scratch,
        compiler_params=pltpu.CompilerParams(
            collective_id=0, has_side_effects=True, vmem_limit_bytes=56 << 20
        ),
        name="expert_relay",
    )(routes_a, scale_a, routes_b, scale_b, x, cot, saved, wgu, wd, jnp.asarray(regroup_matrix(), BF))


def per_device(x_a, routes_a, scale_a, cotangent_b, routes_b, scale_b, saved_b, w_gate_up, w_down_t):
    rows_a, rows_b, perm_a, perm_b = relay_layer(
        routes_a.reshape(1, TOK), scale_a.reshape(1, TOK), routes_b.reshape(1, TOK), scale_b.reshape(1, TOK),
        x_a, cotangent_b, saved_b, w_gate_up, w_down_t,
    )
    put = lambda perm, rows: jnp.einsum("rt,rd->td", perm, rows, preferred_element_type=F32).astype(BF)
    return put(perm_a, rows_a), put(perm_b, rows_b)


def solution(mesh):
    both = ("section", "expert")
    mat, vec = P(both, None), P(both)
    return jax.shard_map(
        per_device, mesh=mesh, in_specs=(mat, vec, vec, mat, vec, vec, mat, mat, mat),
        out_specs=(mat, mat), check_vma=False,
    )
```

```python
import functools

import jax
import jax.numpy as jnp
import numpy as np
from jax import lax
from jax.experimental import pallas as pl
from jax.experimental.pallas import tpu as pltpu
from jax.sharding import PartitionSpec as P

FF = 1024
GROUP = 8
CAP = 12
EXPERTS = 4
SLOTS = EXPERTS * CAP
TOK = 128
EARLY = TOK - SLOTS
D = 7168
SL = D // GROUP
HC = FF // GROUP
ROWS = GROUP * SLOTS
ZROWS = GROUP * CAP
BF = jnp.bfloat16
F32 = jnp.float32
SUM_T = jnp.bfloat16
PIECES = [(0, 16), (16, 32), (48, 32)]
PAIRS = [(2, 0), (2, 1), (1, 0), (1, 1), (3, 0), (3, 1), (0, 1)]


def regroup_matrix():
    row = np.arange(ROWS)
    expert, peer, slot = row // ZROWS, (row % ZROWS) // CAP, row % CAP
    column = peer * SLOTS + expert * CAP + slot
    table = np.zeros((ROWS, ROWS), np.float32)
    table[row, column] = 1.0
    return table


def nt_dot(left, right):
    return lax.dot_general(left, right, (((1,), (1,)), ((), ())), preferred_element_type=F32)


def nn_dot(left, right):
    return jnp.dot(left, right, preferred_element_type=F32)


def iota(shape, dim):
    return lax.broadcasted_iota(jnp.int32, shape, dim)


def slot_positions(routes):
    match = (routes == iota((8, TOK), 0)).astype(F32)
    upper = (iota((TOK, TOK), 0) <= iota((TOK, TOK), 1)).astype(BF)
    rank = nn_dot(match.astype(BF), upper) - 1.0
    counts = jnp.sum(match, axis=1, keepdims=True)
    spare = rank[EXPERTS : EXPERTS + 1] - EARLY
    placed = jnp.zeros((1, TOK), F32)
    leftover = jnp.zeros((1, TOK), F32)
    before = jnp.zeros((1, 1), F32)
    for expert in range(EXPERTS):
        own = match[expert : expert + 1]
        count = counts[expert : expert + 1]
        placed = placed + own * (CAP * expert + rank[expert : expert + 1])
        after = before + (CAP - count)
        inside = (spare >= before) & (spare < after)
        leftover = leftover + jnp.where(inside, CAP * expert + count + (spare - before), 0.0)
        before = after
    outside = jnp.where(spare < 0.0, spare + TOK, leftover)
    return placed + match[EXPERTS : EXPERTS + 1] * outside


def slot_matrix(routes, scale):
    pos = slot_positions(routes)
    hit = iota((TOK, TOK), 0).astype(F32) == pos
    kept = jnp.where(routes < EXPERTS, scale, 0.0)
    column = jnp.sum(jnp.where(hit, kept, 0.0), axis=1, keepdims=True)
    eye = iota((TOK, TOK), 0) == iota((TOK, TOK), 1)
    row = jnp.sum(jnp.where(eye, column, 0.0), axis=0, keepdims=True)
    return hit.astype(BF), row


def kernel(
    routes_a, scale_a, routes_b, scale_b, x_hbm, cot_hbm, saved_hbm, wgu_hbm, wd_hbm, regroup_hbm,
    rows_a, rows_b, perm_a, perm_b,
    x_v, cot_v, saved_v, wgu, wd, regroup,
    pm_a, pm_b, sc_out, sc_in,
    pk_a, pk_b, early_a, early_b,
    r1_a, r1_b, s2_a, s2_b, r2_a, r2_b,
    ps_a, ps_b, sib_a, sib_b, sum_a, sum_b, rs_a, rs_b,
    h_a, g_b, eo_a, eo_b, r3_a, r3_b, s4_a, s4_b, rl_a, rl_b,
    load_sem,
    sc_ss, sc_rs, d1a_ss, d1a_rs, d1b_ss, d1b_rs, d2a_ss, d2a_rs, d2b_ss, d2b_rs,
    sba_ss, sba_rs, sbb_ss, sbb_rs, rsa_ss, rsa_rs, rsb_ss, rsb_rs, aga_ss, aga_rs, agb_ss, agb_rs,
    rta_ss, rta_rs, rtb_ss, rtb_rs, fa_ss, fa_rs, fb_ss, fb_rs, e_ss, e_rs, rl_ss, rl_rs,
):
    section = lax.axis_index("section")
    place = lax.axis_index("expert")
    layer = place // GROUP
    me = place % GROUP
    y = me // 2
    core = me % 2
    n_sec = lax.axis_size("section")
    ahead = (section + 1) % n_sec
    behind = (section + n_sec - 1) % n_sec

    x = section % 4
    edges = {0: x == 3, 1: x == 0}

    def sec_at(step):
        return (section + step + n_sec) % n_sec

    def peer(pair):
        return ((y + pair[0]) % 4) * 2 + (core + pair[1]) % 2

    def plane_dev(pair):
        return (section, layer * GROUP + peer(pair))

    def depth(step):
        return (layer + step) % EXPERTS

    def depth_dev(step):
        return (section, depth(step) * GROUP + me)

    def remote(src, dst, ss, rs, dev):
        return pltpu.make_async_remote_copy(
            src_ref=src, dst_ref=dst, send_sem=ss, recv_sem=rs,
            device_id=dev, device_id_type=pl.DeviceIdType.MESH,
        )

    barrier = pltpu.get_barrier_semaphore()
    greeted = [plane_dev(pair) for pair in PAIRS] + [depth_dev(step) for step in (1, 2, 3)]
    greeted += [(sec_at(step), place) for step in range(1, 8)]
    for other in range(1, GROUP):
        greeted.append((ahead, layer * GROUP + (me + other) % GROUP))
        greeted.append((behind, layer * GROUP + (me + other) % GROUP))
    for dev in greeted:
        pl.semaphore_signal(barrier, 1, device_id=dev, device_id_type=pl.DeviceIdType.MESH)

    loads = []
    for i, (src, dst) in enumerate(
        [(x_hbm, x_v), (cot_hbm, cot_v), (saved_hbm, saved_v), (regroup_hbm, regroup),
         (wgu_hbm, wgu), (wd_hbm, wd)]
    ):
        copy = pltpu.make_async_copy(src, dst, load_sem.at[i])
        if i < 4:
            copy.start()
        loads.append(copy)

    mat_a, row_a = slot_matrix(routes_a[...], scale_a[...])
    mat_b, row_b = slot_matrix(routes_b[...], scale_b[...])
    pm_a[...] = mat_a
    pm_b[...] = mat_b
    line = iota((8, TOK), 0)
    sc_out[...] = jnp.where(line == 0, row_a, jnp.where(line == 1, row_b, 0.0))
    sc_in[me] = sc_out[...]

    pending = []
    finals = []
    guarded = []

    def when_send(cond, copy):
        pl.when(cond)(copy.start)
        guarded.append((cond, copy))

    rows_of = {0: rows_a, 1: rows_b}
    early_of = {0: early_a, 1: early_b}
    relay_of = {0: rl_a, 1: rl_b}
    sign = {0: 1, 1: -1}

    def early_copy(b, i, src, step):
        first, size = PIECES[i]
        return remote(src, rows_of[b].at[pl.ds(SLOTS + first, size), :],
                      e_ss.at[b, i], e_rs.at[b, i], (sec_at(step), place))

    def own_piece(b, i):
        first, size = PIECES[i]
        return early_of[b].at[pl.ds(first, size), :]

    def early_start(b):
        copy = early_copy(b, 0, own_piece(b, 0), sign[b])
        copy.start()
        pending.append(copy)
        for i in (1, 2):
            copy = remote(own_piece(b, i), relay_of[b], e_ss.at[b, i], rl_rs.at[b],
                          (sec_at(-i * sign[b]), place))
            when_send(edges[b], copy)

    def early_direct():
        for b in (0, 1):
            for i in (1, 2):
                when_send(jnp.logical_not(edges[b]), early_copy(b, i, own_piece(b, i), sign[b]))
        for b, (src, dst) in enumerate(((pm_a, perm_a), (pm_b, perm_b))):
            copy = remote(src, dst, e_ss.at[b, 3], e_rs.at[b, 3], (sec_at(sign[b]), place))
            copy.start()
            finals.append(copy)
            pending.append(copy)

    def early_relay(b):
        for i in (1, 2):
            there = x == (3 - i if b == 0 else i)
            copy = remote(relay_of[b], rows_of[b].at[pl.ds(SLOTS + PIECES[i][0], PIECES[i][1]), :],
                          rl_ss.at[b], e_rs.at[b, i], (sec_at((i + 1) * sign[b]), place))

            @pl.when(there)
            def _():
                remote(relay_of[b], relay_of[b], rl_ss.at[b], rl_rs.at[b], (sec_at(1), place)).wait_recv()
                copy.start()

            guarded.append((there, copy))

    loads[0].wait()

    @pl.loop(0, GROUP)
    def _(part):
        cols = pl.ds(pl.multiple_of(part * SL, SL), SL)
        packed = nn_dot(pm_a[...], x_v[:, cols]).astype(BF)
        pk_a[part] = packed[:SLOTS]
        early_a[:, cols] = packed[SLOTS:]

    pl.semaphore_wait(barrier, len(greeted))

    def plane_sends(items):
        out = []
        for i, pair in enumerate(PAIRS):
            for src, dst, ss, rs in items(pair):
                copy = remote(src, dst, ss.at[i], rs.at[i], plane_dev(pair))
                copy.start()
                out.append(copy)
                pending.append(copy)
        return out

    in_1a = plane_sends(lambda pair: [
        (pk_a.at[peer(pair)], r1_a.at[me], d1a_ss, d1a_rs),
        (sc_out, sc_in.at[me], sc_ss, sc_rs),
    ])
    early_start(0)
    r1_a[me] = pk_a[me]
    loads[4].start()
    loads[5].start()

    loads[1].wait()
    loads[2].wait()

    @pl.loop(0, GROUP)
    def _(part):
        cols = pl.ds(pl.multiple_of(part * SL, SL), SL)
        packed = nn_dot(pm_b[...], cot_v[:, cols]).astype(BF)
        pk_b[part, :, :SL] = packed[:SLOTS]
        early_b[:, cols] = packed[SLOTS:]
        first = pl.multiple_of(part * HC, HC)
        second = pl.multiple_of(FF + part * HC, HC)
        held = jnp.concatenate([saved_v[:, pl.ds(first, HC)], saved_v[:, pl.ds(second, HC)]], axis=1)
        pk_b[part, :, SL:] = nn_dot(pm_b[:SLOTS, :], held).astype(BF)

    in_1b = plane_sends(lambda pair: [(pk_b.at[peer(pair)], r1_b.at[me], d1b_ss, d1b_rs)])
    early_start(1)
    r1_b[me] = pk_b[me]

    def scale_column(which):
        mask = iota((SLOTS, TOK), 0) == iota((SLOTS, TOK), 1)
        return [
            jnp.sum(jnp.where(mask, sc_in[p, which : which + 1, :], 0.0), axis=1, keepdims=True)
            for p in range(GROUP)
        ]

    def depth_sends(src, dst, ss, rs):
        out = []
        for i, step in enumerate((2, 1, 3)):
            copy = remote(src.at[depth(step)], dst.at[layer], ss.at[i], rs.at[i], depth_dev(step))
            copy.start()
            out.append(copy)
            pending.append(copy)
        return out

    for copy in in_1a:
        copy.wait_recv()
    loads[3].wait()
    moved = nn_dot(regroup[...], r1_a[...].reshape(ROWS, SL)).astype(BF)
    s2_a[...] = moved.reshape(EXPERTS, ZROWS, SL)
    in_2a = depth_sends(s2_a, r2_a, d2a_ss, d2a_rs)
    r2_a[layer] = s2_a[layer]

    for copy in in_1b:
        copy.wait_recv()
    columns = scale_column(1)
    scaled = jnp.concatenate(
        [(columns[p] * r1_b[p, :, :SL].astype(F32)).astype(BF) for p in range(GROUP)], axis=0
    )
    s2_b[:, :, :SL] = nn_dot(regroup[...], scaled).astype(BF).reshape(EXPERTS, ZROWS, SL)
    carried = r1_b[:, :, SL:].reshape(ROWS, 2 * HC)
    s2_b[:, :, SL:] = nn_dot(regroup[...], carried).astype(BF).reshape(EXPERTS, ZROWS, 2 * HC)
    in_2b = depth_sends(s2_b, r2_b, d2b_ss, d2b_rs)
    r2_b[layer] = s2_b[layer]

    early_direct()

    for copy in in_2a:
        copy.wait_recv()
    loads[4].wait()
    loads[5].wait()
    sibling = plane_dev((0, 1))

    def chip_sums(acts, weights, firsts, ps, sib, sums, rs, sib_ss, sib_rs, ss, rs_rs):
        halves = []
        for d in (2, 1, 3, 0):
            chip = (y + d) % 4
            for n, first in enumerate(firsts):
                at = pl.multiple_of(first + chip * (2 * HC), 2 * HC)
                part = nn_dot(acts, weights[:, pl.ds(at, 2 * HC)])
                ps[d, 0, :, n * HC : (n + 1) * HC] = part[:, :HC]
                ps[d, 1, :, n * HC : (n + 1) * HC] = part[:, HC:]
            copy = remote(ps.at[d, 1 - core], sib.at[d], sib_ss.at[d], sib_rs.at[d], sibling)
            copy.start()
            halves.append(copy)
            pending.append(copy)
        out = []
        for k, d in enumerate((2, 1, 3)):
            halves[k].wait_recv()
            sums[k] = (ps[d, core] + sib[d]).astype(SUM_T)
            copy = remote(sums.at[k], rs.at[k], ss.at[k], rs_rs.at[k], plane_dev((d, 0)))
            copy.start()
            out.append(copy)
            pending.append(copy)
        halves[3].wait_recv()
        return out

    def whole(ps, sib, rs):
        total = ps[0, core] + sib[0]
        for k in range(3):
            total = total + rs[k].astype(F32)
        return total

    def gather_sends(ref, ss, rs):
        out = []
        for k, pair in enumerate(((2, 0), (1, 0), (3, 0), (0, 1))):
            copy = remote(ref.at[me], ref.at[me], ss.at[k], rs.at[k], plane_dev(pair))
            copy.start()
            out.append(copy)
            pending.append(copy)
        return out

    def gather_forwards(copies, ref, ss, rs):
        out = [copies[3]]
        for k, d in enumerate((2, 1, 3)):
            copies[k].wait_recv()
            source = ((y + 4 - d) % 4) * 2 + core
            copy = remote(ref.at[source], ref.at[source], ss.at[4 + k], rs.at[4 + k], sibling)
            copy.start()
            out.append(copy)
            pending.append(copy)
        return out

    in_rsa = chip_sums(r2_a[...].reshape(ROWS, SL), wgu, (0, FF), ps_a, sib_a, sum_a, rs_a,
                       sba_ss, sba_rs, rsa_ss, rsa_rs)

    for copy in in_rsa:
        copy.wait_recv()
    total = whole(ps_a, sib_a, rs_a)
    gate, up = total[:, :HC], total[:, HC:]
    h_a[me] = (gate * jax.nn.sigmoid(gate) * up).astype(BF)
    in_aga = gather_sends(h_a, aga_ss, aga_rs)
    in_aga = gather_forwards(in_aga, h_a, aga_ss, aga_rs)

    for copy in in_2b:
        copy.wait_recv()
    early_relay(0)
    in_rsb = chip_sums(r2_b[:, :, :SL].reshape(ROWS, SL), wd, (0,), ps_b, sib_b, sum_b, rs_b,
                       sbb_ss, sbb_rs, rsb_ss, rsb_rs)

    for copy in in_aga:
        copy.wait_recv()
    hidden = jnp.concatenate([h_a[p] for p in range(GROUP)], axis=1)
    for q in range(0, SL, 128):
        out = nt_dot(hidden, wd[q : q + 128, :]).astype(BF)
        eo_a[:, :, q : q + 128] = out.reshape(EXPERTS, ZROWS, 128)
    in_3a = depth_sends(eo_a, r3_a, rta_ss, rta_rs)
    r3_a[layer] = eo_a[layer]

    for copy in in_rsb:
        copy.wait_recv()
    dhid = whole(ps_b, sib_b, rs_b)
    held = r2_b[:, :, SL:].reshape(ROWS, 2 * HC).astype(F32)
    gate, up = held[:, :HC], held[:, HC:]
    sig = jax.nn.sigmoid(gate)
    g_b[me, :, :HC] = (dhid * up * sig * (1.0 + gate * (1.0 - sig))).astype(BF)
    g_b[me, :, HC:] = (dhid * gate * sig).astype(BF)
    in_agb = gather_sends(g_b, agb_ss, agb_rs)
    in_agb = gather_forwards(in_agb, g_b, agb_ss, agb_rs)

    for copy in in_agb:
        copy.wait_recv()
    left = jnp.concatenate([g_b[p, :, :HC] for p in range(GROUP)], axis=1)
    right = jnp.concatenate([g_b[p, :, HC:] for p in range(GROUP)], axis=1)
    for q in range(0, SL, 128):
        out = nt_dot(left, wgu[q : q + 128, :FF]) + nt_dot(right, wgu[q : q + 128, FF:])
        eo_b[:, :, q : q + 128] = out.astype(BF).reshape(EXPERTS, ZROWS, 128)
    in_3b = depth_sends(eo_b, r3_b, rtb_ss, rtb_rs)
    r3_b[layer] = eo_b[layer]
    early_relay(1)

    def last_sends(src, dst, ss, rs, sec):
        lane = pl.multiple_of(me * SL, SL)
        for p in range(GROUP):
            other = (me + p) % GROUP
            copy = remote(
                src.at[other], dst.at[pl.ds(0, SLOTS), pl.ds(lane, SL)],
                ss.at[p], rs.at[p], (sec, layer * GROUP + other),
            )
            copy.start()
            finals.append(copy)
            pending.append(copy)

    def back(ref):
        return lax.dot_general(
            regroup[...], ref[...].reshape(ROWS, SL), (((0,), (0,)), ((), ())),
            preferred_element_type=F32,
        ).reshape(GROUP, SLOTS, SL)

    for copy in in_3a:
        copy.wait_recv()
    columns = scale_column(0)
    came = back(r3_a)
    for p in range(GROUP):
        s4_a[p] = (r1_a[p].astype(F32) + columns[p] * came[p]).astype(BF)

    for copy in in_3b:
        copy.wait_recv()
    last_sends(s4_a, rows_a, fa_ss, fa_rs, ahead)
    came = back(r3_b)
    for p in range(GROUP):
        s4_b[p] = (r1_b[p, :, :SL].astype(F32) + came[p]).astype(BF)
    last_sends(s4_b, rows_b, fb_ss, fb_rs, behind)

    for b in (0, 1):
        for i in range(3):
            finals.append(early_copy(b, i, own_piece(b, i), sign[b]))
    for copy in finals:
        copy.wait_recv()
    for cond, copy in guarded:
        pl.when(cond)(copy.wait_send)
    for copy in pending:
        copy.wait_send()


def relay_layer(routes_a, scale_a, routes_b, scale_b, x, cot, saved, wgu, wd):
    vmem, hbm = pl.BlockSpec(memory_space=pltpu.VMEM), pl.BlockSpec(memory_space=pl.ANY)
    dma = pltpu.SemaphoreType.DMA
    v = pltpu.VMEM
    n = len(PAIRS)
    wide = SL + 2 * HC
    scratch = [
        v((TOK, D), BF), v((TOK, D), BF), v((TOK, 2 * FF), BF), v((SL, 2 * FF), BF), v((SL, FF), BF), v((ROWS, ROWS), BF),
        v((TOK, TOK), BF), v((TOK, TOK), BF), v((8, TOK), F32), v((GROUP, 8, TOK), F32),
        v((GROUP, SLOTS, SL), BF), v((GROUP, SLOTS, wide), BF), v((EARLY, D), BF), v((EARLY, D), BF),
        v((GROUP, SLOTS, SL), BF), v((GROUP, SLOTS, wide), BF),
        v((EXPERTS, ZROWS, SL), BF), v((EXPERTS, ZROWS, wide), BF),
        v((EXPERTS, ZROWS, SL), BF), v((EXPERTS, ZROWS, wide), BF),
        v((4, 2, ROWS, 2 * HC), F32), v((4, 2, ROWS, HC), F32), v((4, ROWS, 2 * HC), F32), v((4, ROWS, HC), F32),
        v((3, ROWS, 2 * HC), SUM_T), v((3, ROWS, HC), SUM_T), v((3, ROWS, 2 * HC), SUM_T), v((3, ROWS, HC), SUM_T),
        v((GROUP, ROWS, HC), BF), v((GROUP, ROWS, 2 * HC), BF),
        v((EXPERTS, ZROWS, SL), BF), v((EXPERTS, ZROWS, SL), BF),
        v((EXPERTS, ZROWS, SL), BF), v((EXPERTS, ZROWS, SL), BF),
        v((GROUP, SLOTS, SL), BF), v((GROUP, SLOTS, SL), BF),
        v((PIECES[1][1], D), BF), v((PIECES[1][1], D), BF),
        dma((6,)),
    ]
    for size in (n, n, n, 3, 3, 4, 4, 3, 3, n, n, 3, 3, GROUP, GROUP, (2, 4), 2):
        shape = size if isinstance(size, tuple) else (size,)
        scratch += [dma(shape), dma(shape)]
    return pl.pallas_call(
        kernel,
        out_shape=[
            jax.ShapeDtypeStruct((TOK, D), BF), jax.ShapeDtypeStruct((TOK, D), BF),
            jax.ShapeDtypeStruct((TOK, TOK), BF), jax.ShapeDtypeStruct((TOK, TOK), BF),
        ],
        in_specs=[vmem] * 4 + [hbm] * 6,
        out_specs=[hbm] * 4,
        scratch_shapes=scratch,
        compiler_params=pltpu.CompilerParams(
            collective_id=0, has_side_effects=True, vmem_limit_bytes=56 << 20
        ),
        name="expert_relay",
    )(routes_a, scale_a, routes_b, scale_b, x, cot, saved, wgu, wd, jnp.asarray(regroup_matrix(), BF))


def per_device(x_a, routes_a, scale_a, cotangent_b, routes_b, scale_b, saved_b, w_gate_up, w_down_t):
    rows_a, rows_b, perm_a, perm_b = relay_layer(
        routes_a.reshape(1, TOK), scale_a.reshape(1, TOK), routes_b.reshape(1, TOK), scale_b.reshape(1, TOK),
        x_a, cotangent_b, saved_b, w_gate_up, w_down_t,
    )
    put = lambda perm, rows: jnp.einsum("rt,rd->td", perm, rows, preferred_element_type=F32).astype(BF)
    return put(perm_a, rows_a), put(perm_b, rows_b)


def solution(mesh):
    both = ("section", "expert")
    mat, vec = P(both, None), P(both)
    return jax.shard_map(
        per_device, mesh=mesh, in_specs=(mat, vec, vec, mat, vec, vec, mat, mat, mat),
        out_specs=(mat, mat), check_vma=False,
    )
```

```python
import functools

import jax
import jax.numpy as jnp
import numpy as np
from jax import lax
from jax.experimental import pallas as pl
from jax.experimental.pallas import tpu as pltpu
from jax.sharding import PartitionSpec as P

FF = 1024
GROUP = 8
CAP = 12
EXPERTS = 4
SLOTS = EXPERTS * CAP
TOK = 128
EARLY = TOK - SLOTS
D = 7168
SL = D // GROUP
HC = FF // GROUP
ROWS = GROUP * SLOTS
ZROWS = GROUP * CAP
BF = jnp.bfloat16
F32 = jnp.float32
SUM_T = jnp.bfloat16
CUTS = [(0, 384), (384, 896)]
PIECES = [(0, 16), (16, 16), (32, 32), (64, 16)]
PAIRS = [(2, 0), (2, 1), (1, 0), (1, 1), (3, 0), (3, 1), (0, 1)]


def regroup_matrix():
    row = np.arange(ROWS)
    expert, peer, slot = row // ZROWS, (row % ZROWS) // CAP, row % CAP
    column = peer * SLOTS + expert * CAP + slot
    table = np.zeros((ROWS, ROWS), np.float32)
    table[row, column] = 1.0
    return table


def nt_dot(left, right):
    return lax.dot_general(left, right, (((1,), (1,)), ((), ())), preferred_element_type=F32)


def nn_dot(left, right):
    return jnp.dot(left, right, preferred_element_type=F32)


def iota(shape, dim):
    return lax.broadcasted_iota(jnp.int32, shape, dim)


def slot_positions(routes):
    match = (routes == iota((8, TOK), 0)).astype(F32)
    upper = (iota((TOK, TOK), 0) <= iota((TOK, TOK), 1)).astype(BF)
    rank = nn_dot(match.astype(BF), upper) - 1.0
    counts = jnp.sum(match, axis=1, keepdims=True)
    spare = rank[EXPERTS : EXPERTS + 1] - EARLY
    placed = jnp.zeros((1, TOK), F32)
    leftover = jnp.zeros((1, TOK), F32)
    before = jnp.zeros((1, 1), F32)
    for expert in range(EXPERTS):
        own = match[expert : expert + 1]
        count = counts[expert : expert + 1]
        placed = placed + own * (CAP * expert + rank[expert : expert + 1])
        after = before + (CAP - count)
        inside = (spare >= before) & (spare < after)
        leftover = leftover + jnp.where(inside, CAP * expert + count + (spare - before), 0.0)
        before = after
    outside = jnp.where(spare < 0.0, spare + TOK, leftover)
    return placed + match[EXPERTS : EXPERTS + 1] * outside


def slot_matrix(routes, scale):
    pos = slot_positions(routes)
    hit = iota((TOK, TOK), 0).astype(F32) == pos
    kept = jnp.where(routes < EXPERTS, scale, 0.0)
    column = jnp.sum(jnp.where(hit, kept, 0.0), axis=1, keepdims=True)
    eye = iota((TOK, TOK), 0) == iota((TOK, TOK), 1)
    row = jnp.sum(jnp.where(eye, column, 0.0), axis=0, keepdims=True)
    return hit.astype(BF), row


def kernel(
    routes_a, scale_a, routes_b, scale_b, x_hbm, cot_hbm, saved_hbm, wgu_hbm, wd_hbm, regroup_hbm,
    rows_a, rows_b, perm_a, perm_b,
    x_v, cot_v, saved_v, wgu, wd, regroup,
    pm_a, pm_b, sc_out, sc_in,
    pk_a, pk_b, early_a, early_b,
    r1_a, r1_b, s2_a, s2_b, r2_a, r2_b,
    ps_a, ps_b, sib_a, sib_b, sum_a, sum_b, rs_a, rs_b,
    h_a, g_b, eo_a, eo_b, r3_a, r3_b, s4_a, s4_b, near_a, near_b, far_a, far_b,
    load_sem,
    sc_ss, sc_rs, d1a_ss, d1a_rs, d1b_ss, d1b_rs, d2a_ss, d2a_rs, d2b_ss, d2b_rs,
    sba_ss, sba_rs, sbb_ss, sbb_rs, rsa_ss, rsa_rs, rsb_ss, rsb_rs, aga_ss, aga_rs, agb_ss, agb_rs,
    rta_ss, rta_rs, rtb_ss, rtb_rs, fa_ss, fa_rs, fb_ss, fb_rs, e_ss, e_rs, rl_ss, rl_rs,
):
    section = lax.axis_index("section")
    place = lax.axis_index("expert")
    layer = place // GROUP
    me = place % GROUP
    y = me // 2
    core = me % 2
    n_sec = lax.axis_size("section")
    ahead = (section + 1) % n_sec
    behind = (section + n_sec - 1) % n_sec

    x = section % 4
    edges = {0: x == 3, 1: x == 0}

    def sec_at(step):
        return (section + step + n_sec) % n_sec

    def peer(pair):
        return ((y + pair[0]) % 4) * 2 + (core + pair[1]) % 2

    def plane_dev(pair):
        return (section, layer * GROUP + peer(pair))

    def depth(step):
        return (layer + step) % EXPERTS

    def depth_dev(step):
        return (section, depth(step) * GROUP + me)

    def remote(src, dst, ss, rs, dev):
        return pltpu.make_async_remote_copy(
            src_ref=src, dst_ref=dst, send_sem=ss, recv_sem=rs,
            device_id=dev, device_id_type=pl.DeviceIdType.MESH,
        )

    barrier = pltpu.get_barrier_semaphore()
    greeted = [plane_dev(pair) for pair in PAIRS] + [depth_dev(step) for step in (1, 2, 3)]
    greeted += [(sec_at(step), place) for step in range(1, 8)]
    for other in range(1, GROUP):
        greeted.append((ahead, layer * GROUP + (me + other) % GROUP))
        greeted.append((behind, layer * GROUP + (me + other) % GROUP))
    for dev in greeted:
        pl.semaphore_signal(barrier, 1, device_id=dev, device_id_type=pl.DeviceIdType.MESH)

    loads = []
    for i, (src, dst) in enumerate(
        [(x_hbm, x_v), (cot_hbm, cot_v), (saved_hbm, saved_v), (regroup_hbm, regroup),
         (wgu_hbm, wgu), (wd_hbm, wd)]
    ):
        copy = pltpu.make_async_copy(src, dst, load_sem.at[i])
        if i < 4:
            copy.start()
        loads.append(copy)

    mat_a, row_a = slot_matrix(routes_a[...], scale_a[...])
    mat_b, row_b = slot_matrix(routes_b[...], scale_b[...])
    pm_a[...] = mat_a
    pm_b[...] = mat_b
    line = iota((8, TOK), 0)
    sc_out[...] = jnp.where(line == 0, row_a, jnp.where(line == 1, row_b, 0.0))
    sc_in[me] = sc_out[...]

    pending = []
    finals = []
    guarded = []

    def when_send(cond, copy):
        pl.when(cond)(copy.start)
        guarded.append((cond, copy))

    rows_of = {0: rows_a, 1: rows_b}
    early_of = {0: early_a, 1: early_b}
    relay_of = {(0, 2): near_a, (0, 3): far_a, (1, 2): near_b, (1, 3): far_b}
    relay_at = {(0, 2): x == 2, (0, 3): x == 1, (1, 2): x == 1, (1, 3): x == 2}
    sign = {0: 1, 1: -1}

    def early_copy(b, i, src, step):
        first, size = PIECES[i]
        return remote(src, rows_of[b].at[pl.ds(SLOTS + first, size), :],
                      e_ss.at[b, i], e_rs.at[b, i], (sec_at(step), place))

    def own_piece(b, i):
        first, size = PIECES[i]
        return early_of[b].at[pl.ds(first, size), :]

    def early_start(b):
        copy = early_copy(b, 0, own_piece(b, 0), sign[b])
        copy.start()
        pending.append(copy)
        for i in (2, 3):
            copy = remote(own_piece(b, i), relay_of[b, i], e_ss.at[b, i], rl_rs.at[b, i],
                          (sec_at((1 - i) * sign[b]), place))
            when_send(edges[b], copy)

    def early_direct():
        for b in (0, 1):
            for i in (1, 2, 3):
                when_send(jnp.logical_not(edges[b]), early_copy(b, i, own_piece(b, i), sign[b]))
        for b, (src, dst) in enumerate(((pm_a, perm_a), (pm_b, perm_b))):
            copy = remote(src, dst, e_ss.at[b, 4], e_rs.at[b, 4], (sec_at(sign[b]), place))
            copy.start()
            finals.append(copy)
            pending.append(copy)

    def early_border():
        for b in (0, 1):
            when_send(edges[b], early_copy(b, 1, own_piece(b, 1), sign[b]))

    def early_relay(i):
        for b in (0, 1):
            buf, there = relay_of[b, i], relay_at[b, i]
            copy = remote(buf, rows_of[b].at[pl.ds(SLOTS + PIECES[i][0], PIECES[i][1]), :],
                          rl_ss.at[b, i], e_rs.at[b, i], (sec_at(i * sign[b]), place))

            @pl.when(there)
            def _():
                remote(buf, buf, rl_ss.at[b, i], rl_rs.at[b, i], (sec_at(1), place)).wait_recv()
                copy.start()

            guarded.append((there, copy))

    loads[0].wait()

    @pl.loop(0, GROUP)
    def _(part):
        cols = pl.ds(pl.multiple_of(part * SL, SL), SL)
        packed = nn_dot(pm_a[...], x_v[:, cols]).astype(BF)
        pk_a[part] = packed[:SLOTS]
        early_a[:, cols] = packed[SLOTS:]

    pl.semaphore_wait(barrier, len(greeted))

    def plane_sends(items):
        out = []
        for i, pair in enumerate(PAIRS):
            for src, dst, ss, rs in items(pair):
                copy = remote(src, dst, ss.at[i], rs.at[i], plane_dev(pair))
                copy.start()
                out.append(copy)
                pending.append(copy)
        return out

    in_1a = plane_sends(lambda pair: [
        (pk_a.at[peer(pair)], r1_a.at[me], d1a_ss, d1a_rs),
        (sc_out, sc_in.at[me], sc_ss, sc_rs),
    ])
    early_start(0)
    r1_a[me] = pk_a[me]
    loads[4].start()
    loads[5].start()

    loads[1].wait()
    loads[2].wait()

    @pl.loop(0, GROUP)
    def _(part):
        cols = pl.ds(pl.multiple_of(part * SL, SL), SL)
        packed = nn_dot(pm_b[...], cot_v[:, cols]).astype(BF)
        pk_b[part, :, :SL] = packed[:SLOTS]
        early_b[:, cols] = packed[SLOTS:]
        first = pl.multiple_of(part * HC, HC)
        second = pl.multiple_of(FF + part * HC, HC)
        held = jnp.concatenate([saved_v[:, pl.ds(first, HC)], saved_v[:, pl.ds(second, HC)]], axis=1)
        pk_b[part, :, SL:] = nn_dot(pm_b[:SLOTS, :], held).astype(BF)

    in_1b = plane_sends(lambda pair: [(pk_b.at[peer(pair)], r1_b.at[me], d1b_ss, d1b_rs)])
    early_start(1)
    r1_b[me] = pk_b[me]

    def scale_column(which):
        mask = iota((SLOTS, TOK), 0) == iota((SLOTS, TOK), 1)
        return [
            jnp.sum(jnp.where(mask, sc_in[p, which : which + 1, :], 0.0), axis=1, keepdims=True)
            for p in range(GROUP)
        ]

    def depth_sends(src, dst, ss, rs, cols=slice(None)):
        out = []
        for i, step in enumerate((2, 1, 3)):
            copy = remote(src.at[depth(step), :, cols], dst.at[layer, :, cols], ss.at[i], rs.at[i], depth_dev(step))
            copy.start()
            out.append(copy)
            pending.append(copy)
        return out

    for copy in in_1a:
        copy.wait_recv()
    loads[3].wait()
    moved = nn_dot(regroup[...], r1_a[...].reshape(ROWS, SL)).astype(BF)
    s2_a[...] = moved.reshape(EXPERTS, ZROWS, SL)
    in_2a = depth_sends(s2_a, r2_a, d2a_ss, d2a_rs)
    r2_a[layer] = s2_a[layer]

    for copy in in_1b:
        copy.wait_recv()
    columns = scale_column(1)
    scaled = jnp.concatenate(
        [(columns[p] * r1_b[p, :, :SL].astype(F32)).astype(BF) for p in range(GROUP)], axis=0
    )
    s2_b[:, :, :SL] = nn_dot(regroup[...], scaled).astype(BF).reshape(EXPERTS, ZROWS, SL)
    carried = r1_b[:, :, SL:].reshape(ROWS, 2 * HC)
    s2_b[:, :, SL:] = nn_dot(regroup[...], carried).astype(BF).reshape(EXPERTS, ZROWS, 2 * HC)
    in_2b = depth_sends(s2_b, r2_b, d2b_ss, d2b_rs)
    r2_b[layer] = s2_b[layer]

    early_direct()

    for copy in in_2a:
        copy.wait_recv()
    loads[4].wait()
    loads[5].wait()
    sibling = plane_dev((0, 1))

    def chip_sums(acts, weights, firsts, ps, sib, sums, rs, sib_ss, sib_rs, ss, rs_rs):
        halves = []
        for d in (2, 1, 3, 0):
            chip = (y + d) % 4
            for n, first in enumerate(firsts):
                at = pl.multiple_of(first + chip * (2 * HC), 2 * HC)
                part = nn_dot(acts, weights[:, pl.ds(at, 2 * HC)])
                ps[d, 0, :, n * HC : (n + 1) * HC] = part[:, :HC]
                ps[d, 1, :, n * HC : (n + 1) * HC] = part[:, HC:]
            copy = remote(ps.at[d, 1 - core], sib.at[d], sib_ss.at[d], sib_rs.at[d], sibling)
            copy.start()
            halves.append(copy)
            pending.append(copy)
        out = []
        for k, d in enumerate((2, 1, 3)):
            halves[k].wait_recv()
            sums[k] = (ps[d, core] + sib[d]).astype(SUM_T)
            copy = remote(sums.at[k], rs.at[k], ss.at[k], rs_rs.at[k], plane_dev((d, 0)))
            copy.start()
            out.append(copy)
            pending.append(copy)
        halves[3].wait_recv()
        return out

    def whole(ps, sib, rs):
        total = ps[0, core] + sib[0]
        for k in range(3):
            total = total + rs[k].astype(F32)
        return total

    def gather_sends(ref, ss, rs):
        out = []
        for k, pair in enumerate(((2, 0), (1, 0), (3, 0), (0, 1))):
            copy = remote(ref.at[me], ref.at[me], ss.at[k], rs.at[k], plane_dev(pair))
            copy.start()
            out.append(copy)
            pending.append(copy)
        return out

    def gather_forwards(copies, ref, ss, rs):
        out = [copies[3]]
        for k, d in enumerate((2, 1, 3)):
            copies[k].wait_recv()
            source = ((y + 4 - d) % 4) * 2 + core
            copy = remote(ref.at[source], ref.at[source], ss.at[4 + k], rs.at[4 + k], sibling)
            copy.start()
            out.append(copy)
            pending.append(copy)
        return out

    in_rsa = chip_sums(r2_a[...].reshape(ROWS, SL), wgu, (0, FF), ps_a, sib_a, sum_a, rs_a,
                       sba_ss, sba_rs, rsa_ss, rsa_rs)

    for copy in in_rsa:
        copy.wait_recv()
    total = whole(ps_a, sib_a, rs_a)
    gate, up = total[:, :HC], total[:, HC:]
    h_a[me] = (gate * jax.nn.sigmoid(gate) * up).astype(BF)
    in_aga = gather_sends(h_a, aga_ss, aga_rs)
    in_aga = gather_forwards(in_aga, h_a, aga_ss, aga_rs)
    early_relay(3)
    early_border()

    for copy in in_2b:
        copy.wait_recv()
    in_rsb = chip_sums(r2_b[:, :, :SL].reshape(ROWS, SL), wd, (0,), ps_b, sib_b, sum_b, rs_b,
                       sbb_ss, sbb_rs, rsb_ss, rsb_rs)

    for copy in in_aga:
        copy.wait_recv()
    hidden = jnp.concatenate([h_a[p] for p in range(GROUP)], axis=1)
    in_3a = []
    for n, (first, last) in enumerate(CUTS):
        for q in range(first, last, 128):
            out = nt_dot(hidden, wd[q : q + 128, :]).astype(BF)
            eo_a[:, :, q : q + 128] = out.reshape(EXPERTS, ZROWS, 128)
        part = pl.ds(first, last - first)
        in_3a += depth_sends(eo_a, r3_a, rta_ss.at[n], rta_rs.at[n], part)
    r3_a[layer] = eo_a[layer]

    for copy in in_rsb:
        copy.wait_recv()
    dhid = whole(ps_b, sib_b, rs_b)
    held = r2_b[:, :, SL:].reshape(ROWS, 2 * HC).astype(F32)
    gate, up = held[:, :HC], held[:, HC:]
    sig = jax.nn.sigmoid(gate)
    g_b[me, :, :HC] = (dhid * up * sig * (1.0 + gate * (1.0 - sig))).astype(BF)
    g_b[me, :, HC:] = (dhid * gate * sig).astype(BF)
    in_agb = gather_sends(g_b, agb_ss, agb_rs)
    in_agb = gather_forwards(in_agb, g_b, agb_ss, agb_rs)

    for copy in in_agb:
        copy.wait_recv()
    left = jnp.concatenate([g_b[p, :, :HC] for p in range(GROUP)], axis=1)
    right = jnp.concatenate([g_b[p, :, HC:] for p in range(GROUP)], axis=1)
    in_3b = []
    for n, (first, last) in enumerate(CUTS):
        for q in range(first, last, 128):
            out = nt_dot(left, wgu[q : q + 128, :FF]) + nt_dot(right, wgu[q : q + 128, FF:])
            eo_b[:, :, q : q + 128] = out.astype(BF).reshape(EXPERTS, ZROWS, 128)
        part = pl.ds(first, last - first)
        in_3b += depth_sends(eo_b, r3_b, rtb_ss.at[n], rtb_rs.at[n], part)
    r3_b[layer] = eo_b[layer]

    def last_sends(src, dst, ss, rs, sec):
        lane = pl.multiple_of(me * SL, SL)
        for p in range(GROUP):
            other = (me + p) % GROUP
            copy = remote(
                src.at[other], dst.at[pl.ds(0, SLOTS), pl.ds(lane, SL)],
                ss.at[p], rs.at[p], (sec, layer * GROUP + other),
            )
            copy.start()
            finals.append(copy)
            pending.append(copy)

    def back(ref):
        return lax.dot_general(
            regroup[...], ref[...].reshape(ROWS, SL), (((0,), (0,)), ((), ())),
            preferred_element_type=F32,
        ).reshape(GROUP, SLOTS, SL)

    for copy in in_3a:
        copy.wait_recv()
    columns = scale_column(0)
    came = back(r3_a)
    for p in range(GROUP):
        s4_a[p] = (r1_a[p].astype(F32) + columns[p] * came[p]).astype(BF)

    for copy in in_3b:
        copy.wait_recv()
    last_sends(s4_a, rows_a, fa_ss, fa_rs, ahead)
    early_relay(2)
    came = back(r3_b)
    for p in range(GROUP):
        s4_b[p] = (r1_b[p, :, :SL].astype(F32) + came[p]).astype(BF)
    last_sends(s4_b, rows_b, fb_ss, fb_rs, behind)

    for b in (0, 1):
        for i in range(4):
            finals.append(early_copy(b, i, own_piece(b, i), sign[b]))
    for copy in finals:
        copy.wait_recv()
    for cond, copy in guarded:
        pl.when(cond)(copy.wait_send)
    for copy in pending:
        copy.wait_send()


def relay_layer(routes_a, scale_a, routes_b, scale_b, x, cot, saved, wgu, wd):
    vmem, hbm = pl.BlockSpec(memory_space=pltpu.VMEM), pl.BlockSpec(memory_space=pl.ANY)
    dma = pltpu.SemaphoreType.DMA
    v = pltpu.VMEM
    n = len(PAIRS)
    wide = SL + 2 * HC
    scratch = [
        v((TOK, D), BF), v((TOK, D), BF), v((TOK, 2 * FF), BF), v((SL, 2 * FF), BF), v((SL, FF), BF), v((ROWS, ROWS), BF),
        v((TOK, TOK), BF), v((TOK, TOK), BF), v((8, TOK), F32), v((GROUP, 8, TOK), F32),
        v((GROUP, SLOTS, SL), BF), v((GROUP, SLOTS, wide), BF), v((EARLY, D), BF), v((EARLY, D), BF),
        v((GROUP, SLOTS, SL), BF), v((GROUP, SLOTS, wide), BF),
        v((EXPERTS, ZROWS, SL), BF), v((EXPERTS, ZROWS, wide), BF),
        v((EXPERTS, ZROWS, SL), BF), v((EXPERTS, ZROWS, wide), BF),
        v((4, 2, ROWS, 2 * HC), F32), v((4, 2, ROWS, HC), F32), v((4, ROWS, 2 * HC), F32), v((4, ROWS, HC), F32),
        v((3, ROWS, 2 * HC), SUM_T), v((3, ROWS, HC), SUM_T), v((3, ROWS, 2 * HC), SUM_T), v((3, ROWS, HC), SUM_T),
        v((GROUP, ROWS, HC), BF), v((GROUP, ROWS, 2 * HC), BF),
        v((EXPERTS, ZROWS, SL), BF), v((EXPERTS, ZROWS, SL), BF),
        v((EXPERTS, ZROWS, SL), BF), v((EXPERTS, ZROWS, SL), BF),
        v((GROUP, SLOTS, SL), BF), v((GROUP, SLOTS, SL), BF),
        v((PIECES[2][1], D), BF), v((PIECES[2][1], D), BF), v((PIECES[3][1], D), BF), v((PIECES[3][1], D), BF),
        dma((6,)),
    ]
    for size in (n, n, n, 3, 3, 4, 4, 3, 3, n, n, (2, 3), (2, 3), GROUP, GROUP, (2, 5), (2, 4)):
        shape = size if isinstance(size, tuple) else (size,)
        scratch += [dma(shape), dma(shape)]
    return pl.pallas_call(
        kernel,
        out_shape=[
            jax.ShapeDtypeStruct((TOK, D), BF), jax.ShapeDtypeStruct((TOK, D), BF),
            jax.ShapeDtypeStruct((TOK, TOK), BF), jax.ShapeDtypeStruct((TOK, TOK), BF),
        ],
        in_specs=[vmem] * 4 + [hbm] * 6,
        out_specs=[hbm] * 4,
        scratch_shapes=scratch,
        compiler_params=pltpu.CompilerParams(
            collective_id=0, has_side_effects=True, vmem_limit_bytes=56 << 20
        ),
        name="expert_relay",
    )(routes_a, scale_a, routes_b, scale_b, x, cot, saved, wgu, wd, jnp.asarray(regroup_matrix(), BF))


def per_device(x_a, routes_a, scale_a, cotangent_b, routes_b, scale_b, saved_b, w_gate_up, w_down_t):
    rows_a, rows_b, perm_a, perm_b = relay_layer(
        routes_a.reshape(1, TOK), scale_a.reshape(1, TOK), routes_b.reshape(1, TOK), scale_b.reshape(1, TOK),
        x_a, cotangent_b, saved_b, w_gate_up, w_down_t,
    )
    put = lambda perm, rows: jnp.einsum("rt,rd->td", perm, rows, preferred_element_type=F32).astype(BF)
    return put(perm_a, rows_a), put(perm_b, rows_b)


def solution(mesh):
    both = ("section", "expert")
    mat, vec = P(both, None), P(both)
    return jax.shard_map(
        per_device, mesh=mesh, in_specs=(mat, vec, vec, mat, vec, vec, mat, mat, mat),
        out_specs=(mat, mat), check_vma=False,
    )
```

```python
import functools

import jax
import jax.numpy as jnp
import numpy as np
from jax import lax
from jax.experimental import pallas as pl
from jax.experimental.pallas import tpu as pltpu
from jax.sharding import PartitionSpec as P

FF = 1024
GROUP = 8
CAP = 12
EXPERTS = 4
SLOTS = EXPERTS * CAP
TOK = 128
EARLY = TOK - SLOTS
D = 7168
SL = D // GROUP
HC = FF // GROUP
ROWS = GROUP * SLOTS
ZROWS = GROUP * CAP
BF = jnp.bfloat16
F32 = jnp.float32
SUM_T = jnp.bfloat16
CUTS = [(0, 384), (384, 896)]
PIECES = [(0, 16), (16, 16), (32, 32), (64, 16)]
PAIRS = [(2, 0), (2, 1), (1, 0), (1, 1), (3, 0), (3, 1), (0, 1)]


def regroup_matrix():
    row = np.arange(ROWS)
    expert, peer, slot = row // ZROWS, (row % ZROWS) // CAP, row % CAP
    column = peer * SLOTS + expert * CAP + slot
    table = np.zeros((ROWS, ROWS), np.float32)
    table[row, column] = 1.0
    return table


def nt_dot(left, right):
    return lax.dot_general(left, right, (((1,), (1,)), ((), ())), preferred_element_type=F32)


def nn_dot(left, right):
    return jnp.dot(left, right, preferred_element_type=F32)


def iota(shape, dim):
    return lax.broadcasted_iota(jnp.int32, shape, dim)


def slot_positions(routes):
    match = (routes == iota((8, TOK), 0)).astype(F32)
    upper = (iota((TOK, TOK), 0) <= iota((TOK, TOK), 1)).astype(BF)
    rank = nn_dot(match.astype(BF), upper) - 1.0
    counts = jnp.sum(match, axis=1, keepdims=True)
    spare = rank[EXPERTS : EXPERTS + 1] - EARLY
    placed = jnp.zeros((1, TOK), F32)
    leftover = jnp.zeros((1, TOK), F32)
    before = jnp.zeros((1, 1), F32)
    for expert in range(EXPERTS):
        own = match[expert : expert + 1]
        count = counts[expert : expert + 1]
        placed = placed + own * (CAP * expert + rank[expert : expert + 1])
        after = before + (CAP - count)
        inside = (spare >= before) & (spare < after)
        leftover = leftover + jnp.where(inside, CAP * expert + count + (spare - before), 0.0)
        before = after
    outside = jnp.where(spare < 0.0, spare + TOK, leftover)
    return placed + match[EXPERTS : EXPERTS + 1] * outside


def slot_matrix(routes, scale):
    pos = slot_positions(routes)
    hit = iota((TOK, TOK), 0).astype(F32) == pos
    kept = jnp.where(routes < EXPERTS, scale, 0.0)
    column = jnp.sum(jnp.where(hit, kept, 0.0), axis=1, keepdims=True)
    eye = iota((TOK, TOK), 0) == iota((TOK, TOK), 1)
    row = jnp.sum(jnp.where(eye, column, 0.0), axis=0, keepdims=True)
    return hit.astype(BF), row


def kernel(
    routes_a, scale_a, routes_b, scale_b, x_hbm, cot_hbm, saved_hbm, wgu_hbm, wd_hbm, regroup_hbm,
    rows_a, rows_b, perm_a, perm_b,
    x_v, cot_v, saved_v, wgu, wd, regroup,
    pm_a, pm_b, sc_out, sc_in,
    pk_a, pk_b, early_a, early_b,
    r1_a, r1_b, s2_a, s2_b, r2_a, r2_b,
    ps_a, ps_b, sib_a, sib_b, sum_a, sum_b, rs_a, rs_b,
    h_a, g_b, eo_a, eo_b, r3_a, r3_b, s4_a, s4_b, near_a, near_b, far_a, far_b,
    load_sem,
    sc_ss, sc_rs, d1a_ss, d1a_rs, d1b_ss, d1b_rs, d2a_ss, d2a_rs, d2b_ss, d2b_rs,
    sba_ss, sba_rs, sbb_ss, sbb_rs, rsa_ss, rsa_rs, rsb_ss, rsb_rs, aga_ss, aga_rs, agb_ss, agb_rs,
    rta_ss, rta_rs, rtb_ss, rtb_rs, fa_ss, fa_rs, fb_ss, fb_rs, e_ss, e_rs, rl_ss, rl_rs,
):
    section = lax.axis_index("section")
    place = lax.axis_index("expert")
    layer = place // GROUP
    me = place % GROUP
    y = me // 2
    core = me % 2
    n_sec = lax.axis_size("section")
    ahead = (section + 1) % n_sec
    behind = (section + n_sec - 1) % n_sec

    x = section % 4
    edges = {0: x == 3, 1: x == 0}

    def sec_at(step):
        return (section + step + n_sec) % n_sec

    def peer(pair):
        return ((y + pair[0]) % 4) * 2 + (core + pair[1]) % 2

    def plane_dev(pair):
        return (section, layer * GROUP + peer(pair))

    def depth(step):
        return (layer + step) % EXPERTS

    def depth_dev(step):
        return (section, depth(step) * GROUP + me)

    def remote(src, dst, ss, rs, dev):
        return pltpu.make_async_remote_copy(
            src_ref=src, dst_ref=dst, send_sem=ss, recv_sem=rs,
            device_id=dev, device_id_type=pl.DeviceIdType.MESH,
        )

    barrier = pltpu.get_barrier_semaphore()
    greeted = [plane_dev(pair) for pair in PAIRS] + [depth_dev(step) for step in (1, 2, 3)]
    greeted += [(sec_at(step), place) for step in range(1, 8)]
    for other in range(1, GROUP):
        greeted.append((ahead, layer * GROUP + (me + other) % GROUP))
        greeted.append((behind, layer * GROUP + (me + other) % GROUP))
    for dev in greeted:
        pl.semaphore_signal(barrier, 1, device_id=dev, device_id_type=pl.DeviceIdType.MESH)

    loads = []
    for i, (src, dst) in enumerate(
        [(x_hbm, x_v), (cot_hbm, cot_v), (saved_hbm, saved_v), (regroup_hbm, regroup),
         (wgu_hbm, wgu), (wd_hbm, wd)]
    ):
        copy = pltpu.make_async_copy(src, dst, load_sem.at[i])
        if i < 4:
            copy.start()
        loads.append(copy)

    mat_a, row_a = slot_matrix(routes_a[...], scale_a[...])
    mat_b, row_b = slot_matrix(routes_b[...], scale_b[...])
    pm_a[...] = mat_a
    pm_b[...] = mat_b
    line = iota((8, TOK), 0)
    sc_out[...] = jnp.where(line == 0, row_a, jnp.where(line == 1, row_b, 0.0))
    sc_in[me] = sc_out[...]

    pending = []
    finals = []
    guarded = []

    def when_send(cond, copy):
        pl.when(cond)(copy.start)
        guarded.append((cond, copy))

    rows_of = {0: rows_a, 1: rows_b}
    early_of = {0: early_a, 1: early_b}
    relay_of = {(0, 2): near_a, (0, 3): far_a, (1, 2): near_b, (1, 3): far_b}
    relay_at = {(0, 2): x == 2, (0, 3): x == 1, (1, 2): x == 1, (1, 3): x == 2}
    sign = {0: 1, 1: -1}

    def early_copy(b, i, src, step):
        first, size = PIECES[i]
        return remote(src, rows_of[b].at[pl.ds(SLOTS + first, size), :],
                      e_ss.at[b, i], e_rs.at[b, i], (sec_at(step), place))

    def own_piece(b, i):
        first, size = PIECES[i]
        return early_of[b].at[pl.ds(first, size), :]

    def early_start(b):
        copy = early_copy(b, 0, own_piece(b, 0), sign[b])
        copy.start()
        pending.append(copy)
        for i in (2, 3):
            copy = remote(own_piece(b, i), relay_of[b, i], e_ss.at[b, i], rl_rs.at[b, i],
                          (sec_at((1 - i) * sign[b]), place))
            when_send(edges[b], copy)

    def early_direct():
        for b in (0, 1):
            for i in (1, 2, 3):
                when_send(jnp.logical_not(edges[b]), early_copy(b, i, own_piece(b, i), sign[b]))
        for b, (src, dst) in enumerate(((pm_a, perm_a), (pm_b, perm_b))):
            copy = remote(src, dst, e_ss.at[b, 4], e_rs.at[b, 4], (sec_at(sign[b]), place))
            copy.start()
            finals.append(copy)
            pending.append(copy)

    def early_border():
        for b in (0, 1):
            when_send(edges[b], early_copy(b, 1, own_piece(b, 1), sign[b]))

    def early_relay(i):
        for b in (0, 1):
            buf, there = relay_of[b, i], relay_at[b, i]
            copy = remote(buf, rows_of[b].at[pl.ds(SLOTS + PIECES[i][0], PIECES[i][1]), :],
                          rl_ss.at[b, i], e_rs.at[b, i], (sec_at(i * sign[b]), place))

            @pl.when(there)
            def _():
                remote(buf, buf, rl_ss.at[b, i], rl_rs.at[b, i], (sec_at(1), place)).wait_recv()
                copy.start()

            guarded.append((there, copy))

    loads[0].wait()

    @pl.loop(0, GROUP)
    def _(part):
        cols = pl.ds(pl.multiple_of(part * SL, SL), SL)
        packed = nn_dot(pm_a[...], x_v[:, cols]).astype(BF)
        pk_a[part] = packed[:SLOTS]
        early_a[:, cols] = packed[SLOTS:]

    pl.semaphore_wait(barrier, len(greeted))

    def plane_sends(items):
        out = []
        for i, pair in enumerate(PAIRS):
            for src, dst, ss, rs in items(pair):
                copy = remote(src, dst, ss.at[i], rs.at[i], plane_dev(pair))
                copy.start()
                out.append(copy)
                pending.append(copy)
        return out

    in_1a = plane_sends(lambda pair: [
        (pk_a.at[peer(pair)], r1_a.at[me], d1a_ss, d1a_rs),
        (sc_out, sc_in.at[me], sc_ss, sc_rs),
    ])
    early_start(0)
    r1_a[me] = pk_a[me]
    loads[4].start()
    loads[5].start()

    loads[1].wait()
    loads[2].wait()

    @pl.loop(0, GROUP)
    def _(part):
        cols = pl.ds(pl.multiple_of(part * SL, SL), SL)
        packed = nn_dot(pm_b[...], cot_v[:, cols]).astype(BF)
        pk_b[part, :, :SL] = packed[:SLOTS]
        early_b[:, cols] = packed[SLOTS:]
        first = pl.multiple_of(part * HC, HC)
        second = pl.multiple_of(FF + part * HC, HC)
        held = jnp.concatenate([saved_v[:, pl.ds(first, HC)], saved_v[:, pl.ds(second, HC)]], axis=1)
        pk_b[part, :, SL:] = nn_dot(pm_b[:SLOTS, :], held).astype(BF)

    in_1b = plane_sends(lambda pair: [(pk_b.at[peer(pair)], r1_b.at[me], d1b_ss, d1b_rs)])
    early_start(1)
    r1_b[me] = pk_b[me]

    def scale_column(which):
        mask = iota((SLOTS, TOK), 0) == iota((SLOTS, TOK), 1)
        return [
            jnp.sum(jnp.where(mask, sc_in[p, which : which + 1, :], 0.0), axis=1, keepdims=True)
            for p in range(GROUP)
        ]

    def depth_sends(src, dst, ss, rs, cols=slice(None)):
        out = []
        for i, step in enumerate((2, 1, 3)):
            copy = remote(src.at[depth(step), :, cols], dst.at[layer, :, cols], ss.at[i], rs.at[i], depth_dev(step))
            copy.start()
            out.append(copy)
            pending.append(copy)
        return out

    for copy in in_1a:
        copy.wait_recv()
    loads[3].wait()
    moved = nn_dot(regroup[...], r1_a[...].reshape(ROWS, SL)).astype(BF)
    s2_a[...] = moved.reshape(EXPERTS, ZROWS, SL)
    in_2a = depth_sends(s2_a, r2_a, d2a_ss, d2a_rs)
    r2_a[layer] = s2_a[layer]

    for copy in in_1b:
        copy.wait_recv()
    columns = scale_column(1)
    scaled = jnp.concatenate(
        [(columns[p] * r1_b[p, :, :SL].astype(F32)).astype(BF) for p in range(GROUP)], axis=0
    )
    s2_b[:, :, :SL] = nn_dot(regroup[...], scaled).astype(BF).reshape(EXPERTS, ZROWS, SL)
    carried = r1_b[:, :, SL:].reshape(ROWS, 2 * HC)
    s2_b[:, :, SL:] = nn_dot(regroup[...], carried).astype(BF).reshape(EXPERTS, ZROWS, 2 * HC)
    in_2b = depth_sends(s2_b, r2_b, d2b_ss, d2b_rs)
    r2_b[layer] = s2_b[layer]

    early_direct()

    for copy in in_2a:
        copy.wait_recv()
    loads[4].wait()
    loads[5].wait()
    sibling = plane_dev((0, 1))

    def chip_sums(acts, weights, firsts, ps, sib, sums, rs, sib_ss, sib_rs, ss, rs_rs):
        halves = []
        for d in (2, 1, 3, 0):
            chip = (y + d) % 4
            for n, first in enumerate(firsts):
                at = pl.multiple_of(first + chip * (2 * HC), 2 * HC)
                part = nn_dot(acts, weights[:, pl.ds(at, 2 * HC)])
                ps[d, 0, :, n * HC : (n + 1) * HC] = part[:, :HC]
                ps[d, 1, :, n * HC : (n + 1) * HC] = part[:, HC:]
            copy = remote(ps.at[d, 1 - core], sib.at[d], sib_ss.at[d], sib_rs.at[d], sibling)
            copy.start()
            halves.append(copy)
            pending.append(copy)
        out = []
        for k, d in enumerate((2, 1, 3)):
            halves[k].wait_recv()
            sums[k] = (ps[d, core] + sib[d]).astype(SUM_T)
            copy = remote(sums.at[k], rs.at[k], ss.at[k], rs_rs.at[k], plane_dev((d, 0)))
            copy.start()
            out.append(copy)
            pending.append(copy)
        halves[3].wait_recv()
        return out

    def whole(ps, sib, rs):
        total = ps[0, core] + sib[0]
        for k in range(3):
            total = total + rs[k].astype(F32)
        return total

    def gather_sends(ref, ss, rs):
        out = []
        for k, pair in enumerate(((2, 0), (1, 0), (3, 0), (0, 1))):
            copy = remote(ref.at[me], ref.at[me], ss.at[k], rs.at[k], plane_dev(pair))
            copy.start()
            out.append(copy)
            pending.append(copy)
        return out

    def gather_forwards(copies, ref, ss, rs):
        out = [copies[3]]
        for k, d in enumerate((2, 1, 3)):
            copies[k].wait_recv()
            source = ((y + 4 - d) % 4) * 2 + core
            copy = remote(ref.at[source], ref.at[source], ss.at[4 + k], rs.at[4 + k], sibling)
            copy.start()
            out.append(copy)
            pending.append(copy)
        return out

    in_rsa = chip_sums(r2_a[...].reshape(ROWS, SL), wgu, (0, FF), ps_a, sib_a, sum_a, rs_a,
                       sba_ss, sba_rs, rsa_ss, rsa_rs)

    for copy in in_rsa:
        copy.wait_recv()
    total = whole(ps_a, sib_a, rs_a)
    gate, up = total[:, :HC], total[:, HC:]
    h_a[me] = (gate * jax.nn.sigmoid(gate) * up).astype(BF)
    in_aga = gather_sends(h_a, aga_ss, aga_rs)
    in_aga = gather_forwards(in_aga, h_a, aga_ss, aga_rs)
    early_relay(3)
    early_border()

    for copy in in_2b:
        copy.wait_recv()
    in_rsb = chip_sums(r2_b[:, :, :SL].reshape(ROWS, SL), wd, (0,), ps_b, sib_b, sum_b, rs_b,
                       sbb_ss, sbb_rs, rsb_ss, rsb_rs)

    for copy in in_aga:
        copy.wait_recv()
    hidden = jnp.concatenate([h_a[p] for p in range(GROUP)], axis=1)
    in_3a = []
    for n, (first, last) in enumerate(CUTS):
        for q in range(first, last, 128):
            out = nt_dot(hidden, wd[q : q + 128, :]).astype(BF)
            eo_a[:, :, q : q + 128] = out.reshape(EXPERTS, ZROWS, 128)
        part = pl.ds(first, last - first)
        in_3a += depth_sends(eo_a, r3_a, rta_ss.at[n], rta_rs.at[n], part)
    r3_a[layer] = eo_a[layer]

    for copy in in_rsb:
        copy.wait_recv()
    dhid = whole(ps_b, sib_b, rs_b)
    held = r2_b[:, :, SL:].reshape(ROWS, 2 * HC).astype(F32)
    gate, up = held[:, :HC], held[:, HC:]
    sig = jax.nn.sigmoid(gate)
    g_b[me, :, :HC] = (dhid * up * sig * (1.0 + gate * (1.0 - sig))).astype(BF)
    g_b[me, :, HC:] = (dhid * gate * sig).astype(BF)
    in_agb = gather_sends(g_b, agb_ss, agb_rs)
    in_agb = gather_forwards(in_agb, g_b, agb_ss, agb_rs)
    early_relay(2)

    for copy in in_agb:
        copy.wait_recv()
    left = jnp.concatenate([g_b[p, :, :HC] for p in range(GROUP)], axis=1)
    right = jnp.concatenate([g_b[p, :, HC:] for p in range(GROUP)], axis=1)
    in_3b = []
    for n, (first, last) in enumerate(CUTS):
        for q in range(first, last, 128):
            out = nt_dot(left, wgu[q : q + 128, :FF]) + nt_dot(right, wgu[q : q + 128, FF:])
            eo_b[:, :, q : q + 128] = out.astype(BF).reshape(EXPERTS, ZROWS, 128)
        part = pl.ds(first, last - first)
        in_3b += depth_sends(eo_b, r3_b, rtb_ss.at[n], rtb_rs.at[n], part)
    r3_b[layer] = eo_b[layer]

    def last_sends(src, dst, ss, rs, sec):
        lane = pl.multiple_of(me * SL, SL)
        for p in range(GROUP):
            other = (me + p) % GROUP
            copy = remote(
                src.at[other], dst.at[pl.ds(0, SLOTS), pl.ds(lane, SL)],
                ss.at[p], rs.at[p], (sec, layer * GROUP + other),
            )
            copy.start()
            finals.append(copy)
            pending.append(copy)

    def back(ref):
        return lax.dot_general(
            regroup[...], ref[...].reshape(ROWS, SL), (((0,), (0,)), ((), ())),
            preferred_element_type=F32,
        ).reshape(GROUP, SLOTS, SL)

    for copy in in_3a:
        copy.wait_recv()
    columns = scale_column(0)
    came = back(r3_a)
    for p in range(GROUP):
        s4_a[p] = (r1_a[p].astype(F32) + columns[p] * came[p]).astype(BF)

    for copy in in_3b:
        copy.wait_recv()
    last_sends(s4_a, rows_a, fa_ss, fa_rs, ahead)
    came = back(r3_b)
    for p in range(GROUP):
        s4_b[p] = (r1_b[p, :, :SL].astype(F32) + came[p]).astype(BF)
    last_sends(s4_b, rows_b, fb_ss, fb_rs, behind)

    for b in (0, 1):
        for i in range(4):
            finals.append(early_copy(b, i, own_piece(b, i), sign[b]))
    for copy in finals:
        copy.wait_recv()
    for cond, copy in guarded:
        pl.when(cond)(copy.wait_send)
    for copy in pending:
        copy.wait_send()


def relay_layer(routes_a, scale_a, routes_b, scale_b, x, cot, saved, wgu, wd):
    vmem, hbm = pl.BlockSpec(memory_space=pltpu.VMEM), pl.BlockSpec(memory_space=pl.ANY)
    dma = pltpu.SemaphoreType.DMA
    v = pltpu.VMEM
    n = len(PAIRS)
    wide = SL + 2 * HC
    scratch = [
        v((TOK, D), BF), v((TOK, D), BF), v((TOK, 2 * FF), BF), v((SL, 2 * FF), BF), v((SL, FF), BF), v((ROWS, ROWS), BF),
        v((TOK, TOK), BF), v((TOK, TOK), BF), v((8, TOK), F32), v((GROUP, 8, TOK), F32),
        v((GROUP, SLOTS, SL), BF), v((GROUP, SLOTS, wide), BF), v((EARLY, D), BF), v((EARLY, D), BF),
        v((GROUP, SLOTS, SL), BF), v((GROUP, SLOTS, wide), BF),
        v((EXPERTS, ZROWS, SL), BF), v((EXPERTS, ZROWS, wide), BF),
        v((EXPERTS, ZROWS, SL), BF), v((EXPERTS, ZROWS, wide), BF),
        v((4, 2, ROWS, 2 * HC), F32), v((4, 2, ROWS, HC), F32), v((4, ROWS, 2 * HC), F32), v((4, ROWS, HC), F32),
        v((3, ROWS, 2 * HC), SUM_T), v((3, ROWS, HC), SUM_T), v((3, ROWS, 2 * HC), SUM_T), v((3, ROWS, HC), SUM_T),
        v((GROUP, ROWS, HC), BF), v((GROUP, ROWS, 2 * HC), BF),
        v((EXPERTS, ZROWS, SL), BF), v((EXPERTS, ZROWS, SL), BF),
        v((EXPERTS, ZROWS, SL), BF), v((EXPERTS, ZROWS, SL), BF),
        v((GROUP, SLOTS, SL), BF), v((GROUP, SLOTS, SL), BF),
        v((PIECES[2][1], D), BF), v((PIECES[2][1], D), BF), v((PIECES[3][1], D), BF), v((PIECES[3][1], D), BF),
        dma((6,)),
    ]
    for size in (n, n, n, 3, 3, 4, 4, 3, 3, n, n, (2, 3), (2, 3), GROUP, GROUP, (2, 5), (2, 4)):
        shape = size if isinstance(size, tuple) else (size,)
        scratch += [dma(shape), dma(shape)]
    return pl.pallas_call(
        kernel,
        out_shape=[
            jax.ShapeDtypeStruct((TOK, D), BF), jax.ShapeDtypeStruct((TOK, D), BF),
            jax.ShapeDtypeStruct((TOK, TOK), BF), jax.ShapeDtypeStruct((TOK, TOK), BF),
        ],
        in_specs=[vmem] * 4 + [hbm] * 6,
        out_specs=[hbm] * 4,
        scratch_shapes=scratch,
        compiler_params=pltpu.CompilerParams(
            collective_id=0, has_side_effects=True, vmem_limit_bytes=56 << 20
        ),
        name="expert_relay",
    )(routes_a, scale_a, routes_b, scale_b, x, cot, saved, wgu, wd, jnp.asarray(regroup_matrix(), BF))


def per_device(x_a, routes_a, scale_a, cotangent_b, routes_b, scale_b, saved_b, w_gate_up, w_down_t):
    rows_a, rows_b, perm_a, perm_b = relay_layer(
        routes_a.reshape(1, TOK), scale_a.reshape(1, TOK), routes_b.reshape(1, TOK), scale_b.reshape(1, TOK),
        x_a, cotangent_b, saved_b, w_gate_up, w_down_t,
    )
    put = lambda perm, rows: jnp.einsum("rt,rd->td", perm, rows, preferred_element_type=F32).astype(BF)
    return put(perm_a, rows_a), put(perm_b, rows_b)


def solution(mesh):
    both = ("section", "expert")
    mat, vec = P(both, None), P(both)
    return jax.shard_map(
        per_device, mesh=mesh, in_specs=(mat, vec, vec, mat, vec, vec, mat, mat, mat),
        out_specs=(mat, mat), check_vma=False,
    )
```

```python
import functools

import jax
import jax.numpy as jnp
import numpy as np
from jax import lax
from jax.experimental import pallas as pl
from jax.experimental.pallas import tpu as pltpu
from jax.sharding import PartitionSpec as P

FF = 1024
GROUP = 8
CAP = 12
EXPERTS = 4
SLOTS = EXPERTS * CAP
TOK = 128
EARLY = TOK - SLOTS
D = 7168
SL = D // GROUP
HC = FF // GROUP
ROWS = GROUP * SLOTS
ZROWS = GROUP * CAP
BF = jnp.bfloat16
F32 = jnp.float32
SUM_T = jnp.bfloat16
CUTS = [(0, 384), (384, 896)]
PIECES = [(0, 16), (16, 16), (32, 32), (64, 16)]
PAIRS = [(2, 0), (2, 1), (1, 0), (1, 1), (3, 0), (3, 1), (0, 1)]


def regroup_matrix():
    row = np.arange(ROWS)
    expert, peer, slot = row // ZROWS, (row % ZROWS) // CAP, row % CAP
    column = peer * SLOTS + expert * CAP + slot
    table = np.zeros((ROWS, ROWS), np.float32)
    table[row, column] = 1.0
    return table


def nt_dot(left, right):
    return lax.dot_general(left, right, (((1,), (1,)), ((), ())), preferred_element_type=F32)


def nn_dot(left, right):
    return jnp.dot(left, right, preferred_element_type=F32)


def iota(shape, dim):
    return lax.broadcasted_iota(jnp.int32, shape, dim)


def slot_positions(routes):
    match = (routes == iota((8, TOK), 0)).astype(F32)
    upper = (iota((TOK, TOK), 0) <= iota((TOK, TOK), 1)).astype(BF)
    rank = nn_dot(match.astype(BF), upper) - 1.0
    counts = jnp.sum(match, axis=1, keepdims=True)
    spare = rank[EXPERTS : EXPERTS + 1] - EARLY
    placed = jnp.zeros((1, TOK), F32)
    leftover = jnp.zeros((1, TOK), F32)
    before = jnp.zeros((1, 1), F32)
    for expert in range(EXPERTS):
        own = match[expert : expert + 1]
        count = counts[expert : expert + 1]
        placed = placed + own * (CAP * expert + rank[expert : expert + 1])
        after = before + (CAP - count)
        inside = (spare >= before) & (spare < after)
        leftover = leftover + jnp.where(inside, CAP * expert + count + (spare - before), 0.0)
        before = after
    outside = jnp.where(spare < 0.0, spare + TOK, leftover)
    return placed + match[EXPERTS : EXPERTS + 1] * outside


def slot_matrix(routes, scale):
    pos = slot_positions(routes)
    hit = iota((TOK, TOK), 0).astype(F32) == pos
    kept = jnp.where(routes < EXPERTS, scale, 0.0)
    column = jnp.sum(jnp.where(hit, kept, 0.0), axis=1, keepdims=True)
    eye = iota((TOK, TOK), 0) == iota((TOK, TOK), 1)
    row = jnp.sum(jnp.where(eye, column, 0.0), axis=0, keepdims=True)
    return hit.astype(BF), row


def kernel(
    routes_a, scale_a, routes_b, scale_b, x_hbm, cot_hbm, saved_hbm, wgu_hbm, wd_hbm, regroup_hbm,
    rows_a, rows_b, perm_a, perm_b,
    x_v, cot_v, saved_v, wgu, wd, regroup,
    pm_a, pm_b, sc_out, sc_in,
    pk_a, pk_b, early_a, early_b,
    r1_a, r1_b, s2_a, s2_b, r2_a, r2_b,
    ps_a, ps_b, sib_a, sib_b, sum_a, sum_b, rs_a, rs_b,
    h_a, g_b, eo_a, eo_b, r3_a, r3_b, s4_a, s4_b, near_a, near_b, far_a, far_b,
    load_sem,
    sc_ss, sc_rs, d1a_ss, d1a_rs, d1b_ss, d1b_rs, d2a_ss, d2a_rs, d2b_ss, d2b_rs,
    sba_ss, sba_rs, sbb_ss, sbb_rs, rsa_ss, rsa_rs, rsb_ss, rsb_rs, aga_ss, aga_rs, agb_ss, agb_rs,
    rta_ss, rta_rs, rtb_ss, rtb_rs, fa_ss, fa_rs, fb_ss, fb_rs, e_ss, e_rs, rl_ss, rl_rs,
):
    section = lax.axis_index("section")
    place = lax.axis_index("expert")
    layer = place // GROUP
    me = place % GROUP
    y = me // 2
    core = me % 2
    n_sec = lax.axis_size("section")
    ahead = (section + 1) % n_sec
    behind = (section + n_sec - 1) % n_sec

    x = section % 4
    edges = {0: x == 3, 1: x == 0}

    def sec_at(step):
        return (section + step + n_sec) % n_sec

    def peer(pair):
        return ((y + pair[0]) % 4) * 2 + (core + pair[1]) % 2

    def plane_dev(pair):
        return (section, layer * GROUP + peer(pair))

    def depth(step):
        return (layer + step) % EXPERTS

    def depth_dev(step):
        return (section, depth(step) * GROUP + me)

    def remote(src, dst, ss, rs, dev):
        return pltpu.make_async_remote_copy(
            src_ref=src, dst_ref=dst, send_sem=ss, recv_sem=rs,
            device_id=dev, device_id_type=pl.DeviceIdType.MESH,
        )

    barrier = pltpu.get_barrier_semaphore()
    greeted = [plane_dev(pair) for pair in PAIRS] + [depth_dev(step) for step in (1, 2, 3)]
    greeted += [(sec_at(step), place) for step in range(1, 8)]
    for other in range(1, GROUP):
        greeted.append((ahead, layer * GROUP + (me + other) % GROUP))
        greeted.append((behind, layer * GROUP + (me + other) % GROUP))
    for dev in greeted:
        pl.semaphore_signal(barrier, 1, device_id=dev, device_id_type=pl.DeviceIdType.MESH)

    loads = []
    for i, (src, dst) in enumerate(
        [(x_hbm, x_v), (cot_hbm, cot_v), (saved_hbm, saved_v), (regroup_hbm, regroup),
         (wgu_hbm, wgu), (wd_hbm, wd)]
    ):
        copy = pltpu.make_async_copy(src, dst, load_sem.at[i])
        if i < 4:
            copy.start()
        loads.append(copy)

    mat_a, row_a = slot_matrix(routes_a[...], scale_a[...])
    mat_b, row_b = slot_matrix(routes_b[...], scale_b[...])
    pm_a[...] = mat_a
    pm_b[...] = mat_b
    line = iota((8, TOK), 0)
    sc_out[...] = jnp.where(line == 0, row_a, jnp.where(line == 1, row_b, 0.0))
    sc_in[me] = sc_out[...]

    pending = []
    finals = []
    guarded = []

    def when_send(cond, copy):
        pl.when(cond)(copy.start)
        guarded.append((cond, copy))

    rows_of = {0: rows_a, 1: rows_b}
    early_of = {0: early_a, 1: early_b}
    relay_of = {(0, 2): near_a, (0, 3): far_a, (1, 2): near_b, (1, 3): far_b}
    relay_at = {(0, 2): x == 2, (0, 3): x == 1, (1, 2): x == 1, (1, 3): x == 2}
    sign = {0: 1, 1: -1}

    def early_copy(b, i, src, step):
        first, size = PIECES[i]
        return remote(src, rows_of[b].at[pl.ds(SLOTS + first, size), :],
                      e_ss.at[b, i], e_rs.at[b, i], (sec_at(step), place))

    def own_piece(b, i):
        first, size = PIECES[i]
        return early_of[b].at[pl.ds(first, size), :]

    def early_start(b):
        copy = early_copy(b, 0, own_piece(b, 0), sign[b])
        copy.start()
        pending.append(copy)
        for i in (2, 3):
            copy = remote(own_piece(b, i), relay_of[b, i], e_ss.at[b, i], rl_rs.at[b, i],
                          (sec_at((1 - i) * sign[b]), place))
            when_send(edges[b], copy)

    def early_direct():
        for b in (0, 1):
            for i in (1, 2, 3):
                when_send(jnp.logical_not(edges[b]), early_copy(b, i, own_piece(b, i), sign[b]))
        for b, (src, dst) in enumerate(((pm_a, perm_a), (pm_b, perm_b))):
            copy = remote(src, dst, e_ss.at[b, 4], e_rs.at[b, 4], (sec_at(sign[b]), place))
            copy.start()
            finals.append(copy)
            pending.append(copy)

    def early_border():
        for b in (0, 1):
            when_send(edges[b], early_copy(b, 1, own_piece(b, 1), sign[b]))

    def early_relay(i):
        for b in (0, 1):
            buf, there = relay_of[b, i], relay_at[b, i]
            copy = remote(buf, rows_of[b].at[pl.ds(SLOTS + PIECES[i][0], PIECES[i][1]), :],
                          rl_ss.at[b, i], e_rs.at[b, i], (sec_at(i * sign[b]), place))

            @pl.when(there)
            def _():
                remote(buf, buf, rl_ss.at[b, i], rl_rs.at[b, i], (sec_at(1), place)).wait_recv()
                copy.start()

            guarded.append((there, copy))

    loads[0].wait()

    @pl.loop(0, GROUP)
    def _(part):
        cols = pl.ds(pl.multiple_of(part * SL, SL), SL)
        packed = nn_dot(pm_a[...], x_v[:, cols]).astype(BF)
        pk_a[part] = packed[:SLOTS]
        early_a[:, cols] = packed[SLOTS:]

    pl.semaphore_wait(barrier, len(greeted))

    def plane_sends(items):
        out = []
        for i, pair in enumerate(PAIRS):
            for src, dst, ss, rs in items(pair):
                copy = remote(src, dst, ss.at[i], rs.at[i], plane_dev(pair))
                copy.start()
                out.append(copy)
                pending.append(copy)
        return out

    in_1a = plane_sends(lambda pair: [
        (pk_a.at[peer(pair)], r1_a.at[me], d1a_ss, d1a_rs),
        (sc_out, sc_in.at[me], sc_ss, sc_rs),
    ])
    early_start(0)
    r1_a[me] = pk_a[me]
    loads[4].start()
    loads[5].start()

    loads[1].wait()
    loads[2].wait()

    @pl.loop(0, GROUP)
    def _(part):
        cols = pl.ds(pl.multiple_of(part * SL, SL), SL)
        packed = nn_dot(pm_b[...], cot_v[:, cols]).astype(BF)
        pk_b[part, :, :SL] = packed[:SLOTS]
        early_b[:, cols] = packed[SLOTS:]
        first = pl.multiple_of(part * HC, HC)
        second = pl.multiple_of(FF + part * HC, HC)
        held = jnp.concatenate([saved_v[:, pl.ds(first, HC)], saved_v[:, pl.ds(second, HC)]], axis=1)
        pk_b[part, :, SL:] = nn_dot(pm_b[:SLOTS, :], held).astype(BF)

    in_1b = plane_sends(lambda pair: [(pk_b.at[peer(pair)], r1_b.at[me], d1b_ss, d1b_rs)])
    early_start(1)
    r1_b[me] = pk_b[me]

    def scale_column(which):
        mask = iota((SLOTS, TOK), 0) == iota((SLOTS, TOK), 1)
        return [
            jnp.sum(jnp.where(mask, sc_in[p, which : which + 1, :], 0.0), axis=1, keepdims=True)
            for p in range(GROUP)
        ]

    def depth_sends(src, dst, ss, rs, cols=slice(None)):
        out = []
        for i, step in enumerate((2, 1, 3)):
            copy = remote(src.at[depth(step), :, cols], dst.at[layer, :, cols], ss.at[i], rs.at[i], depth_dev(step))
            copy.start()
            out.append(copy)
            pending.append(copy)
        return out

    for copy in in_1a:
        copy.wait_recv()
    loads[3].wait()
    moved = nn_dot(regroup[...], r1_a[...].reshape(ROWS, SL)).astype(BF)
    s2_a[...] = moved.reshape(EXPERTS, ZROWS, SL)
    in_2a = depth_sends(s2_a, r2_a, d2a_ss, d2a_rs)
    r2_a[layer] = s2_a[layer]

    for copy in in_1b:
        copy.wait_recv()
    columns = scale_column(1)
    scaled = jnp.concatenate(
        [(columns[p] * r1_b[p, :, :SL].astype(F32)).astype(BF) for p in range(GROUP)], axis=0
    )
    s2_b[:, :, :SL] = nn_dot(regroup[...], scaled).astype(BF).reshape(EXPERTS, ZROWS, SL)
    carried = r1_b[:, :, SL:].reshape(ROWS, 2 * HC)
    s2_b[:, :, SL:] = nn_dot(regroup[...], carried).astype(BF).reshape(EXPERTS, ZROWS, 2 * HC)
    in_2b = depth_sends(s2_b, r2_b, d2b_ss, d2b_rs)
    r2_b[layer] = s2_b[layer]

    early_direct()

    for copy in in_2a:
        copy.wait_recv()
    loads[4].wait()
    loads[5].wait()
    sibling = plane_dev((0, 1))

    def chip_sums(acts, weights, firsts, ps, sib, sums, rs, sib_ss, sib_rs, ss, rs_rs):
        halves = []
        for d in (2, 1, 3, 0):
            chip = (y + d) % 4
            for n, first in enumerate(firsts):
                at = pl.multiple_of(first + chip * (2 * HC), 2 * HC)
                part = nn_dot(acts, weights[:, pl.ds(at, 2 * HC)])
                ps[d, 0, :, n * HC : (n + 1) * HC] = part[:, :HC]
                ps[d, 1, :, n * HC : (n + 1) * HC] = part[:, HC:]
            copy = remote(ps.at[d, 1 - core], sib.at[d], sib_ss.at[d], sib_rs.at[d], sibling)
            copy.start()
            halves.append(copy)
            pending.append(copy)
        out = []
        for k, d in enumerate((2, 1, 3)):
            halves[k].wait_recv()
            sums[k] = (ps[d, core] + sib[d]).astype(SUM_T)
            copy = remote(sums.at[k], rs.at[k], ss.at[k], rs_rs.at[k], plane_dev((d, 0)))
            copy.start()
            out.append(copy)
            pending.append(copy)
        halves[3].wait_recv()
        return out

    def whole(ps, sib, rs):
        total = ps[0, core] + sib[0]
        for k in range(3):
            total = total + rs[k].astype(F32)
        return total

    def gather_sends(ref, ss, rs):
        out = []
        for k, pair in enumerate(((2, 0), (1, 0), (3, 0), (0, 1))):
            copy = remote(ref.at[me], ref.at[me], ss.at[k], rs.at[k], plane_dev(pair))
            copy.start()
            out.append(copy)
            pending.append(copy)
        return out

    def gather_forwards(copies, ref, ss, rs):
        out = [copies[3]]
        for k, d in enumerate((2, 1, 3)):
            copies[k].wait_recv()
            source = ((y + 4 - d) % 4) * 2 + core
            copy = remote(ref.at[source], ref.at[source], ss.at[4 + k], rs.at[4 + k], sibling)
            copy.start()
            out.append(copy)
            pending.append(copy)
        return out

    in_rsa = chip_sums(r2_a[...].reshape(ROWS, SL), wgu, (0, FF), ps_a, sib_a, sum_a, rs_a,
                       sba_ss, sba_rs, rsa_ss, rsa_rs)

    for copy in in_rsa:
        copy.wait_recv()
    total = whole(ps_a, sib_a, rs_a)
    gate, up = total[:, :HC], total[:, HC:]
    h_a[me] = (gate * jax.nn.sigmoid(gate) * up).astype(BF)
    in_aga = gather_sends(h_a, aga_ss, aga_rs)
    in_aga = gather_forwards(in_aga, h_a, aga_ss, aga_rs)
    early_relay(3)
    early_border()

    for copy in in_2b:
        copy.wait_recv()
    in_rsb = chip_sums(r2_b[:, :, :SL].reshape(ROWS, SL), wd, (0,), ps_b, sib_b, sum_b, rs_b,
                       sbb_ss, sbb_rs, rsb_ss, rsb_rs)

    for copy in in_aga:
        copy.wait_recv()
    hidden = jnp.concatenate([h_a[p] for p in range(GROUP)], axis=1)
    in_3a = []
    for n, (first, last) in enumerate(CUTS):
        for q in range(first, last, 128):
            out = nt_dot(hidden, wd[q : q + 128, :]).astype(BF)
            eo_a[:, :, q : q + 128] = out.reshape(EXPERTS, ZROWS, 128)
        part = pl.ds(first, last - first)
        in_3a += depth_sends(eo_a, r3_a, rta_ss.at[n], rta_rs.at[n], part)
    r3_a[layer] = eo_a[layer]

    for copy in in_rsb:
        copy.wait_recv()
    dhid = whole(ps_b, sib_b, rs_b)
    held = r2_b[:, :, SL:].reshape(ROWS, 2 * HC).astype(F32)
    gate, up = held[:, :HC], held[:, HC:]
    sig = jax.nn.sigmoid(gate)
    g_b[me, :, :HC] = (dhid * up * sig * (1.0 + gate * (1.0 - sig))).astype(BF)
    g_b[me, :, HC:] = (dhid * gate * sig).astype(BF)
    in_agb = gather_sends(g_b, agb_ss, agb_rs)
    in_agb = gather_forwards(in_agb, g_b, agb_ss, agb_rs)
    early_relay(2)

    for copy in in_agb:
        copy.wait_recv()
    left = jnp.concatenate([g_b[p, :, :HC] for p in range(GROUP)], axis=1)
    right = jnp.concatenate([g_b[p, :, HC:] for p in range(GROUP)], axis=1)
    in_3b = []
    for n, (first, last) in enumerate(CUTS):
        for q in range(first, last, 128):
            out = nt_dot(left, wgu[q : q + 128, :FF]) + nt_dot(right, wgu[q : q + 128, FF:])
            eo_b[:, :, q : q + 128] = out.astype(BF).reshape(EXPERTS, ZROWS, 128)
        part = pl.ds(first, last - first)
        in_3b += depth_sends(eo_b, r3_b, rtb_ss.at[n], rtb_rs.at[n], part)
    r3_b[layer] = eo_b[layer]

    def last_sends(src, dst, ss, rs, sec, cond=None):
        lane = pl.multiple_of(me * SL, SL)
        for p in range(GROUP):
            other = (me + p) % GROUP
            copy = remote(
                src.at[other], dst.at[pl.ds(0, SLOTS), pl.ds(lane, SL)],
                ss.at[p], rs.at[p], (sec, layer * GROUP + other),
            )
            if cond is None:
                copy.start()
            else:
                pl.when(cond)(copy.start)
            if cond is not edges[0]:
                finals.append(copy)
                pending.append(copy)

    def back(ref):
        return lax.dot_general(
            regroup[...], ref[...].reshape(ROWS, SL), (((0,), (0,)), ((), ())),
            preferred_element_type=F32,
        ).reshape(GROUP, SLOTS, SL)

    for copy in in_3a:
        copy.wait_recv()
    columns = scale_column(0)
    came = back(r3_a)
    for p in range(GROUP):
        s4_a[p] = (r1_a[p].astype(F32) + columns[p] * came[p]).astype(BF)

    last_sends(s4_a, rows_a, fa_ss, fa_rs, ahead, jnp.logical_not(edges[0]))

    for copy in in_3b:
        copy.wait_recv()
    last_sends(s4_a, rows_a, fa_ss, fa_rs, ahead, edges[0])
    came = back(r3_b)
    for p in range(GROUP):
        s4_b[p] = (r1_b[p, :, :SL].astype(F32) + came[p]).astype(BF)
    last_sends(s4_b, rows_b, fb_ss, fb_rs, behind)

    for b in (0, 1):
        for i in range(4):
            finals.append(early_copy(b, i, own_piece(b, i), sign[b]))
    for copy in finals:
        copy.wait_recv()
    for cond, copy in guarded:
        pl.when(cond)(copy.wait_send)
    for copy in pending:
        copy.wait_send()


def relay_layer(routes_a, scale_a, routes_b, scale_b, x, cot, saved, wgu, wd):
    vmem, hbm = pl.BlockSpec(memory_space=pltpu.VMEM), pl.BlockSpec(memory_space=pl.ANY)
    dma = pltpu.SemaphoreType.DMA
    v = pltpu.VMEM
    n = len(PAIRS)
    wide = SL + 2 * HC
    scratch = [
        v((TOK, D), BF), v((TOK, D), BF), v((TOK, 2 * FF), BF), v((SL, 2 * FF), BF), v((SL, FF), BF), v((ROWS, ROWS), BF),
        v((TOK, TOK), BF), v((TOK, TOK), BF), v((8, TOK), F32), v((GROUP, 8, TOK), F32),
        v((GROUP, SLOTS, SL), BF), v((GROUP, SLOTS, wide), BF), v((EARLY, D), BF), v((EARLY, D), BF),
        v((GROUP, SLOTS, SL), BF), v((GROUP, SLOTS, wide), BF),
        v((EXPERTS, ZROWS, SL), BF), v((EXPERTS, ZROWS, wide), BF),
        v((EXPERTS, ZROWS, SL), BF), v((EXPERTS, ZROWS, wide), BF),
        v((4, 2, ROWS, 2 * HC), F32), v((4, 2, ROWS, HC), F32), v((4, ROWS, 2 * HC), F32), v((4, ROWS, HC), F32),
        v((3, ROWS, 2 * HC), SUM_T), v((3, ROWS, HC), SUM_T), v((3, ROWS, 2 * HC), SUM_T), v((3, ROWS, HC), SUM_T),
        v((GROUP, ROWS, HC), BF), v((GROUP, ROWS, 2 * HC), BF),
        v((EXPERTS, ZROWS, SL), BF), v((EXPERTS, ZROWS, SL), BF),
        v((EXPERTS, ZROWS, SL), BF), v((EXPERTS, ZROWS, SL), BF),
        v((GROUP, SLOTS, SL), BF), v((GROUP, SLOTS, SL), BF),
        v((PIECES[2][1], D), BF), v((PIECES[2][1], D), BF), v((PIECES[3][1], D), BF), v((PIECES[3][1], D), BF),
        dma((6,)),
    ]
    for size in (n, n, n, 3, 3, 4, 4, 3, 3, n, n, (2, 3), (2, 3), GROUP, GROUP, (2, 5), (2, 4)):
        shape = size if isinstance(size, tuple) else (size,)
        scratch += [dma(shape), dma(shape)]
    return pl.pallas_call(
        kernel,
        out_shape=[
            jax.ShapeDtypeStruct((TOK, D), BF), jax.ShapeDtypeStruct((TOK, D), BF),
            jax.ShapeDtypeStruct((TOK, TOK), BF), jax.ShapeDtypeStruct((TOK, TOK), BF),
        ],
        in_specs=[vmem] * 4 + [hbm] * 6,
        out_specs=[hbm] * 4,
        scratch_shapes=scratch,
        compiler_params=pltpu.CompilerParams(
            collective_id=0, has_side_effects=True, vmem_limit_bytes=56 << 20
        ),
        name="expert_relay",
    )(routes_a, scale_a, routes_b, scale_b, x, cot, saved, wgu, wd, jnp.asarray(regroup_matrix(), BF))


def token_order_kernel(perm_a, rows_a, perm_b, rows_b, out_a, out_b):
    for perm, rows, out in ((perm_a, rows_a, out_a), (perm_b, rows_b, out_b)):
        out[...] = lax.dot_general(
            perm[...], rows[...], (((0,), (0,)), ((), ())), preferred_element_type=F32
        ).astype(BF)


def token_order(perm_a, rows_a, perm_b, rows_b):
    tile = 1792
    square = pl.BlockSpec((TOK, TOK), lambda i: (0, 0))
    wide = pl.BlockSpec((TOK, tile), lambda i: (0, i))
    return pl.pallas_call(
        token_order_kernel,
        grid=(D // tile,),
        out_shape=[jax.ShapeDtypeStruct((TOK, D), BF)] * 2,
        in_specs=[square, wide, square, wide],
        out_specs=[wide, wide],
        name="token_order",
    )(perm_a, rows_a, perm_b, rows_b)


def per_device(x_a, routes_a, scale_a, cotangent_b, routes_b, scale_b, saved_b, w_gate_up, w_down_t):
    rows_a, rows_b, perm_a, perm_b = relay_layer(
        routes_a.reshape(1, TOK), scale_a.reshape(1, TOK), routes_b.reshape(1, TOK), scale_b.reshape(1, TOK),
        x_a, cotangent_b, saved_b, w_gate_up, w_down_t,
    )
    return token_order(perm_a, rows_a, perm_b, rows_b)


def solution(mesh):
    both = ("section", "expert")
    mat, vec = P(both, None), P(both)
    return jax.shard_map(
        per_device, mesh=mesh, in_specs=(mat, vec, vec, mat, vec, vec, mat, mat, mat),
        out_specs=(mat, mat), check_vma=False,
    )
```
